128 devices in a mesh: trow: 8 (over x_lo, z), tcol: 16 (over y, x_hi, core).
Axes of the slice: x: 4 (x_hi: 2, x_lo: 2; x = x_hi * 2 + x_lo), y: 4, z: 4, core: 2. Of those that a mesh axis runs over, the one named last changes fastest.
Arguments:
- signal: bfloat16 [256, 32768], P(None, ('tcol', 'trow')), may hold values from -6 to 6
- left_factors: bfloat16 [16, 16, 2048, 256], P('trow', 'tcol'), may hold values from -0.09375 to 0.09375
- right_factors: bfloat16 [16, 16, 2048, 256], P('trow', 'tcol'), may hold values from -0.125 to 0.125
- dense_diagonal: bfloat16 [16, 2048, 2048], P('tcol'), may hold values from -0.125 to 0.125
- buckets: int32 [16, 16], P('trow', 'tcol'), may hold values from 0 to 4
Outputs:
- first_out: bfloat16 [256, 32768], P(None, ('trow', 'tcol'))
- second_out: bfloat16 [256, 32768], P(None, ('tcol', 'trow'))
The draws below stay inside these ranges and needn't reach their ends.
Inputs may be any that keep to these rules, and one draw needn't show every extreme that they name: A tile's rank is 16 times two to the power of its bucket; factor columns past the rank are not part of the tile, and the diagonal tiles' buckets are unused.
All inputs are finite; a program needn't handle non-finite values.
Results may differ from the reference program's by a relative error of at most 0.022.
Values may be sent and summed in bfloat16 or wider, within the bound.
No kernel may reach another device: no remote copies, remote signals or barrier semaphores. Data moves between devices by JAX's collectives and lax.ppermute only.
A program may use at most 128 MiB of HBM per device.

```python
import jax
import jax.numpy as jnp
from jax import lax

B = 2048
R = 256
K = 256
NT = 16
N = 32768


def set_ends(values, stream_key, least, high):
    shape = values.shape
    index_at = [jax.random.randint(jax.random.fold_in(stream_key, axis), (), 0, shape[axis]) for axis in range(len(shape))]
    values = values.at[tuple(index_at)].set(least)
    longest = shape.index(max(shape))
    index_at[longest] = (index_at[longest] + 1) % shape[longest]
    return values.at[tuple(index_at)].set(high)


def level_of(key, dims, shards, low, top_value):
    level = 1.0
    for position, blocks in shards:
        steps = jax.random.uniform(jax.random.fold_in(jax.random.fold_in(key, 6), position), (blocks,), jnp.float32, low / len(shards), top_value / len(shards))
        level = level * jnp.repeat(jnp.exp(steps), dims[position] // blocks).reshape((-1,) + (1,) * (len(dims) - 1 - position))
    return level


def normal_values(own_key, shape, scale, reach, cuts=(), kind=jnp.bfloat16):
    drawn = scale * jax.random.normal(own_key, shape, jnp.float32)
    if cuts:
        drawn = drawn * level_of(own_key, shape, cuts, -0.22, 0.18)
    return jnp.clip(drawn, -reach, reach).astype(kind)


def setup_inputs(seed: int = 0) -> dict:
    keys = jax.random.split(jax.random.key(seed), 6)
    signal = normal_values(keys[0], (K, N), 1.0, 6.0, ((1, 128),))
    left_factors = normal_values(keys[1], (NT, NT, B, R), (R * NT) ** -0.5, 0.09375, ((0, 8), (1, 16)))
    right_factors = normal_values(keys[2], (NT, NT, B, R), B ** -0.5, 0.125, ((0, 8), (1, 16)))
    dense_diagonal = normal_values(keys[3], (NT, B, B), B ** -0.5, 0.125, ((0, 16),))
    buckets = set_ends(jax.random.randint(keys[4], (NT, NT), 0, 5), jax.random.fold_in(keys[4], 1), 0, 4).astype(jnp.int32)
    return dict(signal=signal, left_factors=left_factors, right_factors=right_factors, dense_diagonal=dense_diagonal, buckets=buckets)


def reference(signal, left_factors, right_factors, dense_diagonal, buckets):
    kept_rank = jnp.left_shift(jnp.int32(16), buckets)
    off_diagonal = 1.0 - jnp.eye(NT, dtype=jnp.float32)
    rank_mask = (jnp.arange(R, dtype=jnp.int32)[None, None, :] < kept_rank[:, :, None]).astype(jnp.float32) * off_diagonal[:, :, None]
    x_tiles = jnp.transpose(signal.reshape(K, NT, B), (1, 0, 2)).astype(jnp.float32)

    def forward_row(operands):
        left_row, right_row, diag_tile, mask_row, x_own = operands
        coefficients = jnp.einsum("jkb,jbr->jkr", x_tiles, right_row.astype(jnp.float32)) * mask_row[:, None, :]
        coefficients = lax.optimization_barrier(coefficients.astype(jnp.bfloat16)).astype(jnp.float32)
        low_part = jnp.einsum("jkr,jbr->kb", coefficients, left_row.astype(jnp.float32))
        dense_part = jnp.einsum("kc,bc->kb", x_own, diag_tile.astype(jnp.float32))
        return (low_part + dense_part).astype(jnp.bfloat16)

    first_tiles = lax.map(forward_row, (left_factors, right_factors, dense_diagonal, rank_mask, x_tiles))
    first_out = jnp.transpose(first_tiles, (1, 0, 2)).reshape(K, NT * B)
    y_tiles = first_tiles.astype(jnp.float32)

    def transpose_row(running, operands):
        left_row, right_row, mask_row, y_own = operands
        coefficients = jnp.einsum("kb,jbr->jkr", y_own, left_row.astype(jnp.float32)) * mask_row[:, None, :]
        coefficients = lax.optimization_barrier(coefficients.astype(jnp.bfloat16)).astype(jnp.float32)
        return running + jnp.einsum("jkr,jbr->jkb", coefficients, right_row.astype(jnp.float32)), None

    low_total, unused = lax.scan(transpose_row, jnp.zeros((NT, K, B), jnp.float32), (left_factors, right_factors, rank_mask, y_tiles))
    dense_total = jnp.einsum("jkb,jbc->jkc", y_tiles, dense_diagonal.astype(jnp.float32))
    second_tiles = (low_total + dense_total).astype(jnp.bfloat16)
    second_out = jnp.transpose(second_tiles, (1, 0, 2)).reshape(K, NT * B)
    return (first_out, second_out)
```

```python
import functools

import jax
import jax.numpy as jnp
from jax import lax
from jax.experimental import pallas as pl
from jax.experimental.pallas import tpu as pltpu
from jax.sharding import PartitionSpec as P

CHUNKS = 1
PIECE = 256
F32 = jnp.float32
BF16 = jnp.bfloat16
REL = [(d, x) for d in range(4) for x in range(2)]
VMEM = pl.BlockSpec(memory_space=pltpu.VMEM)
SMEM = pl.BlockSpec(memory_space=pltpu.SMEM)


def dot(a, b):
    return lax.dot_general(a, b, (((1,), (0,)), ((), ())), preferred_element_type=F32)


def dot_t(a, b):
    return lax.dot_general(a, b, (((1,), (1,)), ((), ())), preferred_element_type=F32)


def total(parts):
    return functools.reduce(lambda a, b: a + b, parts)


def row_piece(info, rel):
    return (info[0] ^ rel[1]) * 4 + (info[1] ^ rel[0])


def half_piece(info, rel):
    return (info[2] ^ rel[0]) * 2 + (info[3] ^ rel[1])


def rows_of(piece):
    return pl.ds(pl.multiple_of(piece * PIECE, PIECE), PIECE)


def masked(values, rank):
    columns = lax.broadcasted_iota(jnp.int32, values.shape, 1)
    return jnp.where(columns < rank, values, 0.0)


def coeff_kernel(info, *refs):
    x, right, out = refs[:8], refs[8], refs[9]
    for t in range(2):
        acc = total(dot(x[n][...], right[t, rows_of(row_piece(info, rel)), :]) for n, rel in enumerate(REL))
        out[t] = masked(acc, info[4 + t]).astype(BF16)


def diag_kernel(info, *refs):
    x, dense, out = refs[:8], refs[8], refs[9]
    acc = total(dot_t(x[n][...], dense[:, rows_of(row_piece(info, rel))]) for n, rel in enumerate(REL))
    out[...] = acc.astype(BF16)


def term_kernel(info, own, mate, left_own, left_mate, *outs):
    for out, rel in zip(outs, REL):
        piece = half_piece(info, rel)
        tile = piece // 4
        acc = dot_t(own[tile], left_own[piece]) + dot_t(mate[tile], left_mate[piece])
        out[...] = acc.astype(BF16)


def back_kernel(info, *refs):
    y, left_own, left_mate, own, mate = refs[:8], refs[8], refs[9], refs[10], refs[11]
    for half in range(2):
        tile = (info[2] // 2) ^ half
        for left, out in ((left_mate, mate), (left_own, own)):
            out[tile] = total(
                dot(y[n][...], left[half_piece(info, rel)]) for n, rel in enumerate(REL) if rel[0] // 2 == half
            ).astype(out.dtype)


def second_kernel(info, own, mate, right, y_diag, dense, *outs):
    coeff = [masked(own[t] + mate[t].astype(F32), info[4 + t]).astype(BF16) for t in range(2)]
    for out, rel in zip(outs, REL):
        rows = rows_of(row_piece(info, rel))
        acc = dot_t(coeff[0], right[0, rows, :]) + dot_t(coeff[1], right[1, rows, :])
        out[...] = (acc + dot(y_diag[...], dense[:, rows])).astype(BF16)


def call(kernel, name, info, operands, outs, flops, moved):
    return pl.pallas_call(
        kernel,
        name=name,
        out_shape=outs,
        in_specs=[SMEM] + [VMEM] * len(operands),
        out_specs=[VMEM] * len(outs),
        cost_estimate=pl.CostEstimate(flops=flops, bytes_accessed=moved, transcendentals=0),
    )(info, *operands)


def swap(x, axis, bits):
    size = lax.axis_size(axis)
    return lax.ppermute(x, axis, [(i, i ^ bits) for i in range(size)])


def gather(own, axis, ring, side):
    got = {(0, 0): own}
    got[(0, 1)] = swap(own, axis, side)
    for d in (1, 3, 2):
        got[(d, 0)] = swap(own, axis, d * ring)
    for d in (1, 3, 2):
        got[(d, 1)] = swap(got[(0, 1)], axis, d * ring)
    return [got[rel] for rel in REL]


def scatter(pieces, axis, ring, side, extra=()):
    piece = dict(zip(REL, pieces))
    far = [piece[(0, 1)]] + [swap(piece[(d, 1)], axis, d * ring) for d in (1, 3, 2)]
    near = [piece[(0, 0)]] + [swap(piece[(d, 0)], axis, d * ring) for d in (1, 3, 2)]
    crossed = swap(total(v.astype(F32) for v in far).astype(BF16), axis, side)
    return total(v.astype(F32) for v in near + [crossed] + list(extra)).astype(BF16)


def body(signal, left_factors, right_factors, dense_diagonal, buckets):
    trow = lax.axis_index("trow")
    tcol = lax.axis_index("tcol")
    core = tcol % 2
    tile_rows = trow * 2 + jnp.arange(2, dtype=jnp.int32)
    ranks = jnp.where(tile_rows == tcol, 0, jnp.left_shift(jnp.int32(16), buckets[:, 0]))
    info = jnp.concatenate([jnp.stack([trow // 4, trow % 4, tcol // 4, (tcol // 2) % 2]), ranks]).astype(jnp.int32)

    right = right_factors[:, 0]
    left = left_factors.reshape(2, 4, 2, PIECE, PIECE)
    left_own = lax.dynamic_index_in_dim(left, core, 2, keepdims=False).reshape(8, PIECE, PIECE)
    left_sent = lax.dynamic_index_in_dim(left, 1 - core, 2, keepdims=False).reshape(8, PIECE, PIECE)
    left_mate = swap(left_sent, "tcol", 1)
    dense = lax.dynamic_slice_in_dim(dense_diagonal[0], trow * PIECE, PIECE, 0)
    to_owner = [(a * 16 + b, (b // 2) * 16 + (b % 2) * 8 + a) for a in range(8) for b in range(16)]
    from_owner = [(d, s) for s, d in to_owner]

    count = signal.shape[0] // CHUNKS
    unit = 2 * count * PIECE * PIECE
    size = count * PIECE * 2
    piece = jax.ShapeDtypeStruct((count, PIECE), BF16)
    pair = jax.ShapeDtypeStruct((2, count, PIECE), BF16)
    pair_wide = jax.ShapeDtypeStruct((2, count, PIECE), F32)
    firsts, seconds = [], []
    for c in range(CHUNKS):
        x = gather(signal[c * count : (c + 1) * count], "trow", 1, 4)
        (coeff,) = call(coeff_kernel, "coeff", info, [*x, right], [pair], 16 * unit, 10 * size + 2**21)
        coeff_mate = swap(coeff, "tcol", 1)
        (diag,) = call(diag_kernel, "diag", info, [*x, dense], [piece], 8 * unit, 9 * size + 2**20)
        diag = lax.ppermute(diag, ("trow", "tcol"), to_owner)
        terms = call(
            term_kernel, "term", info, [coeff, coeff_mate, left_own, left_mate], [piece] * 8, 16 * unit, 12 * size + 2**21
        )
        first = scatter(terms, "tcol", 4, 2, [diag])
        y = gather(first, "tcol", 4, 2)
        y_diag = lax.ppermute(first, ("trow", "tcol"), from_owner)
        own, mate = call(
            back_kernel, "back", info, [*y, left_own, left_mate], [pair_wide, pair], 16 * unit, 14 * size + 2**21
        )
        mate = swap(mate, "tcol", 1)
        terms = call(
            second_kernel, "second", info, [own, mate, right, y_diag, dense], [piece] * 8, 24 * unit, 15 * size + 3 * 2**20
        )
        second = scatter(terms, "trow", 1, 4)
        firsts.append(first)
        seconds.append(second)
    return (jnp.concatenate(firsts, 0), jnp.concatenate(seconds, 0))


def solution(mesh):
    in_specs = (
        P(None, ("tcol", "trow")),
        P("trow", "tcol", None, None),
        P("trow", "tcol", None, None),
        P("tcol", None, None),
        P("trow", "tcol"),
    )
    out_specs = (P(None, ("trow", "tcol")), P(None, ("tcol", "trow")))
    return jax.shard_map(body, mesh=mesh, in_specs=in_specs, out_specs=out_specs, check_vma=False)
```

```python
import functools

import jax
import jax.numpy as jnp
from jax import lax
from jax.experimental import pallas as pl
from jax.experimental.pallas import tpu as pltpu
from jax.sharding import PartitionSpec as P

PIECE = 256
F32 = jnp.float32
BF16 = jnp.bfloat16
REL = [(d, x) for d in range(4) for x in range(2)]
VMEM = pl.BlockSpec(memory_space=pltpu.VMEM)
SMEM = pl.BlockSpec(memory_space=pltpu.SMEM)


def dot(a, b):
    return lax.dot_general(a, b, (((1,), (0,)), ((), ())), preferred_element_type=F32)


def dot_t(a, b):
    return lax.dot_general(a, b, (((1,), (1,)), ((), ())), preferred_element_type=F32)


def total(parts):
    return functools.reduce(lambda a, b: a + b, parts)


def row_piece(info, rel):
    return (info[0] ^ rel[1]) * 4 + (info[1] ^ rel[0])


def half_piece(info, rel):
    return (info[2] ^ rel[0]) * 2 + (info[3] ^ rel[1])


def rows_of(piece):
    return pl.ds(pl.multiple_of(piece * PIECE, PIECE), PIECE)


def left_rows(info, piece):
    return rows_of((piece % 4) * 2 + info[6])


def masked(values, rank):
    columns = lax.broadcasted_iota(jnp.int32, values.shape, 1)
    return jnp.where(columns < rank, values, 0.0)


def coeff_kernel(info, *refs):
    x, right, out = refs[:8], refs[8], refs[9]
    for t in range(2):
        acc = total(dot(x[n][...], right[t, rows_of(row_piece(info, rel)), :]) for n, rel in enumerate(REL))
        out[t] = masked(acc, info[4 + t]).astype(BF16)


def diag_kernel(for_mate, info, *refs):
    x, dense, out = refs[:8], refs[8], refs[9]
    parity = info[6] ^ for_mate

    @pl.when(info[7] == 1)
    def _():
        for q in range(4):
            rows = rows_of(2 * q + parity)
            acc = total(dot_t(x[n][...], dense[rows, rows_of(row_piece(info, rel))]) for n, rel in enumerate(REL))
            out[q] = acc.astype(out.dtype)


def term_kernel(info, own, mate, left_own, left_mate, dense_own, dense_mate, *outs):
    core = info[6]
    for out, rel in zip(outs, REL):
        piece = half_piece(info, rel)
        tile = piece // 4
        rows = left_rows(info, piece)
        acc = dot_t(own[tile], left_own[tile, rows, :]) + dot_t(mate[tile], left_mate[tile, rows, :])

        @pl.when(info[7] == 0)
        def _():
            out[...] = acc.astype(BF16)

        @pl.when(jnp.logical_and(info[7] == 1, tile == core))
        def _():
            out[...] = (acc + dense_own[piece % 4].astype(F32)).astype(BF16)

        @pl.when(jnp.logical_and(info[7] == 1, tile != core))
        def _():
            out[...] = (acc + dense_mate[piece % 4].astype(F32)).astype(BF16)


def pack_kernel(info, *refs):
    y, out = refs[:8], refs[8]
    for n, rel in enumerate(REL):
        piece = half_piece(info, rel)

        @pl.when(jnp.logical_and(info[7] == 1, piece // 4 != info[6]))
        def _():
            out[piece % 4] = y[n][...]


def back_kernel(info, *refs):
    y, left_own, left_mate, own, mate = refs[:8], refs[8], refs[9], refs[10], refs[11]
    for half in range(2):
        tile = (info[2] // 2) ^ half
        for left, out in ((left_mate, mate), (left_own, own)):
            out[tile] = total(
                dot(y[n][...], left[tile, left_rows(info, half_piece(info, rel)), :])
                for n, rel in enumerate(REL)
                if rel[0] // 2 == half
            ).astype(out.dtype)


def diag_back_kernel(info, *refs):
    y, dense, out = refs[:8], refs[8], refs[9]
    for half in range(2):

        @pl.when(jnp.logical_and(info[7] == 1, (info[2] // 2) ^ half == info[6]))
        def _():
            for p in range(8):
                out[p] = total(
                    dot(y[n][...], dense[left_rows(info, half_piece(info, rel)), p * PIECE : (p + 1) * PIECE])
                    for n, rel in enumerate(REL)
                    if rel[0] // 2 == half
                )


def second_kernel(info, own, mate, right, dense_sum, y_mate, dense, *outs):
    coeff = [masked(own[t] + mate[t].astype(F32), info[4 + t]).astype(BF16) for t in range(2)]
    for out, rel in zip(outs, REL):
        piece = row_piece(info, rel)
        rows = rows_of(piece)
        acc = dot_t(coeff[0], right[0, rows, :]) + dot_t(coeff[1], right[1, rows, :])

        @pl.when(info[7] == 0)
        def _():
            out[...] = acc.astype(BF16)

        @pl.when(info[7] == 1)
        def _():
            rest = total(dot(y_mate[q], dense[rows_of(2 * q + 1 - info[6]), rows]) for q in range(4))
            out[...] = (acc + dense_sum[piece] + rest).astype(BF16)


def call(kernel, name, info, operands, outs, flops, moved):
    return pl.pallas_call(
        kernel,
        name=name,
        out_shape=outs,
        in_specs=[SMEM] + [VMEM] * len(operands),
        out_specs=[VMEM] * len(outs),
        compiler_params=pltpu.CompilerParams(vmem_limit_bytes=16 * 2**20),
        cost_estimate=pl.CostEstimate(flops=flops, bytes_accessed=moved, transcendentals=0),
    )(info, *operands)


def swap(x, axis, bits):
    size = lax.axis_size(axis)
    return lax.ppermute(x, axis, [(i, i ^ bits) for i in range(size)])


def gather(own, axis, ring, side):
    got = {(0, 0): own}
    got[(0, 1)] = swap(own, axis, side)
    got[(2, 0)] = swap(own, axis, 2 * ring)
    got[(1, 0)] = swap(own, axis, ring)
    got[(3, 0)] = swap(own, axis, 3 * ring)
    got[(1, 1)] = swap(got[(0, 1)], axis, ring)
    got[(3, 1)] = swap(got[(0, 1)], axis, 3 * ring)
    got[(2, 1)] = swap(got[(2, 0)], axis, side)
    return [got[rel] for rel in REL]


def add(*parts):
    return total(v.astype(F32) for v in parts).astype(BF16)


def scatter(pieces, axis, ring, side):
    piece = dict(zip(REL, pieces))
    far_1 = swap(piece[(1, 1)], axis, ring)
    far_3 = swap(piece[(3, 1)], axis, 3 * ring)
    far_2 = swap(piece[(2, 1)], axis, side)
    near_1 = swap(piece[(1, 0)], axis, ring)
    near_3 = swap(piece[(3, 0)], axis, 3 * ring)
    near_2 = swap(add(piece[(2, 0)], far_2), axis, 2 * ring)
    crossed = swap(add(piece[(0, 1)], far_1, far_3), axis, side)
    return add(piece[(0, 0)], near_1, near_3, near_2, crossed)


def body(signal, left_factors, right_factors, dense_diagonal, buckets):
    trow = lax.axis_index("trow")
    tcol = lax.axis_index("tcol")
    tile_rows = trow * 2 + jnp.arange(2, dtype=jnp.int32)
    ranks = jnp.where(tile_rows == tcol, 0, jnp.left_shift(jnp.int32(16), buckets[:, 0]))
    place = jnp.stack([trow // 4, trow % 4, tcol // 4, (tcol // 2) % 2])
    owner = (trow == tcol // 2).astype(jnp.int32)
    info = jnp.concatenate([place, ranks, jnp.stack([tcol % 2, owner])]).astype(jnp.int32)

    right = right_factors[:, 0]
    left = left_factors[:, 0]
    dense = dense_diagonal[0]
    left_mate = swap(left, "tcol", 1)
    owners = [((b // 2) * 16 + b, (b // 2) * 16 + (b ^ 1)) for b in range(16)]

    count = signal.shape[0]
    unit = 2 * count * PIECE * PIECE
    size = count * PIECE * 2
    piece = jax.ShapeDtypeStruct((count, PIECE), BF16)
    pair = jax.ShapeDtypeStruct((2, count, PIECE), BF16)
    pair_wide = jax.ShapeDtypeStruct((2, count, PIECE), F32)
    four = jax.ShapeDtypeStruct((4, count, PIECE), BF16)
    eight_wide = jax.ShapeDtypeStruct((8, count, PIECE), F32)

    x = gather(signal, "trow", 1, 4)
    (coeff,) = call(coeff_kernel, "coeff", info, [*x, right], [pair], 16 * unit, 10 * size + 2**21)
    coeff_mate = swap(coeff, "tcol", 1)
    (dense_sent,) = call(functools.partial(diag_kernel, 1), "diag_mate", info, [*x, dense], [four], 32 * unit, 12 * size + 2**23)
    dense_mate = lax.ppermute(dense_sent, ("trow", "tcol"), owners)
    (dense_own,) = call(functools.partial(diag_kernel, 0), "diag_own", info, [*x, dense], [four], 32 * unit, 12 * size + 2**23)
    terms = call(
        term_kernel,
        "term",
        info,
        [coeff, coeff_mate, left, left_mate, dense_own, dense_mate],
        [piece] * 8,
        16 * unit,
        20 * size + 2**21,
    )
    first = scatter(terms, "tcol", 4, 2)
    y = gather(first, "tcol", 4, 2)
    (y_sent,) = call(pack_kernel, "pack", info, y, [four], 0, 12 * size)
    y_mate = lax.ppermute(y_sent, ("trow", "tcol"), owners)
    own, mate = call(back_kernel, "back", info, [*y, left, left_mate], [pair_wide, pair], 16 * unit, 14 * size + 2**21)
    mate = swap(mate, "tcol", 1)
    (dense_sum,) = call(diag_back_kernel, "diag_back", info, [*y, dense], [eight_wide], 32 * unit, 24 * size + 2**22)
    terms = call(
        second_kernel,
        "second",
        info,
        [own, mate, right, dense_sum, y_mate, dense],
        [piece] * 8,
        48 * unit,
        30 * size + 3 * 2**20,
    )
    second = scatter(terms, "trow", 1, 4)
    return (first, second)


def solution(mesh):
    in_specs = (
        P(None, ("tcol", "trow")),
        P("trow", "tcol", None, None),
        P("trow", "tcol", None, None),
        P("tcol", None, None),
        P("trow", "tcol"),
    )
    out_specs = (P(None, ("trow", "tcol")), P(None, ("tcol", "trow")))
    return jax.shard_map(body, mesh=mesh, in_specs=in_specs, out_specs=out_specs, check_vma=False)
```

```python
import functools

import jax
import jax.numpy as jnp
from jax import lax
from jax.experimental import pallas as pl
from jax.experimental.pallas import tpu as pltpu
from jax.sharding import PartitionSpec as P

PIECE = 256
F32 = jnp.float32
BF16 = jnp.bfloat16
REL = [(d, x) for d in range(4) for x in range(2)]
FAR = [(1, 1), (3, 1), (2, 1)]
NEAR = [(1, 0), (3, 0), (2, 0), (0, 1), (0, 0)]
VMEM = pl.BlockSpec(memory_space=pltpu.VMEM)


def dot(a, b):
    return lax.dot_general(a, b, (((1,), (0,)), ((), ())), preferred_element_type=F32)


def dot_t(a, b):
    return lax.dot_general(a, b, (((1,), (1,)), ((), ())), preferred_element_type=F32)


def total(parts):
    return functools.reduce(lambda a, b: a + b, parts)


class Place:
    def __init__(self, buckets=None):
        trow = lax.axis_index("trow")
        tcol = lax.axis_index("tcol")
        self.x_lo, self.z = trow >> 2, trow & 3
        self.y, self.x_hi, self.core = tcol >> 2, (tcol >> 1) & 1, tcol & 1
        self.owner = trow == tcol >> 1
        if buckets is not None:
            self.ranks = [jnp.where(trow * 2 + t == tcol, 0, 16 << buckets[:, t : t + 1]) for t in range(2)]


def row_piece(info, rel):
    return (info.x_lo ^ rel[1]) * 4 + (info.z ^ rel[0])


def half_piece(info, rel):
    return (info.y ^ rel[0]) * 2 + (info.x_hi ^ rel[1])


def rows_of(piece):
    return pl.ds(pl.multiple_of(piece * PIECE, PIECE), PIECE)


def left_rows(info, piece):
    return rows_of((piece % 4) * 2 + info.core)


def masked(values, rank):
    columns = lax.broadcasted_iota(jnp.int32, values.shape, 1)
    return jnp.where(columns < rank, values, 0.0)


def coeff_kernel(buckets, *refs):
    info = Place(buckets)
    x, right, out = refs[:8], refs[8], refs[9]
    for t in range(2):
        acc = total(dot(x[n][...], right[t, rows_of(row_piece(info, rel)), :]) for n, rel in enumerate(REL))
        out[t] = masked(acc, info.ranks[t]).astype(BF16)


def diag_kernel(for_mate, *refs):
    info = Place()
    x, dense, out = refs[:8], refs[8], refs[9]
    parity = info.core ^ for_mate

    @pl.when(info.owner)
    def _():
        for q in range(4):
            rows = rows_of(2 * q + parity)
            acc = total(dot_t(x[n][...], dense[rows, rows_of(row_piece(info, rel))]) for n, rel in enumerate(REL))
            out[q] = acc.astype(out.dtype)


def term_kernel(rels, own, mate, left_own, left_mate, dense_own, dense_mate, *outs):
    info = Place()

    def low(piece):
        tile = piece // 4
        rows = left_rows(info, piece)
        return dot_t(own[tile], left_own[tile, rows, :]) + dot_t(mate[tile], left_mate[tile, rows, :])

    @pl.when(jnp.logical_not(info.owner))
    def _():
        for out, rel in zip(outs, rels):
            out[...] = low(half_piece(info, rel)).astype(BF16)

    @pl.when(info.owner)
    def _():
        for out, rel in zip(outs, rels):
            piece = half_piece(info, rel)
            extra = jnp.where(piece // 4 == info.core, dense_own[piece % 4], dense_mate[piece % 4])
            out[...] = (low(piece) + extra.astype(F32)).astype(BF16)


def pack_kernel(*refs):
    info = Place()
    y, out = refs[:8], refs[8]
    for n, rel in enumerate(REL):
        piece = half_piece(info, rel)

        @pl.when(jnp.logical_and(info.owner, piece // 4 != info.core))
        def _():
            out[piece % 4] = y[n][...]


def back_kernel(*refs):
    info = Place()
    y, left_own, left_mate, own, mate = refs[:8], refs[8], refs[9], refs[10], refs[11]
    for half in range(2):
        tile = (info.y // 2) ^ half
        for left, out in ((left_mate, mate), (left_own, own)):
            out[tile] = total(
                dot(y[n][...], left[tile, left_rows(info, half_piece(info, rel)), :])
                for n, rel in enumerate(REL)
                if rel[0] // 2 == half
            ).astype(out.dtype)


def diag_back_kernel(*refs):
    info = Place()
    y, dense, out = refs[:8], refs[8], refs[9]
    for half in range(2):

        @pl.when(jnp.logical_and(info.owner, (info.y // 2) ^ half == info.core))
        def _():
            for p in range(8):
                out[p] = total(
                    dot(y[n][...], dense[left_rows(info, half_piece(info, rel)), p * PIECE : (p + 1) * PIECE])
                    for n, rel in enumerate(REL)
                    if rel[0] // 2 == half
                )


def second_kernel(rels, buckets, own, mate, right, dense_sum, y_mate, dense, *outs):
    info = Place(buckets)
    coeff = [masked(own[t] + mate[t].astype(F32), info.ranks[t]).astype(BF16) for t in range(2)]

    def low(rows):
        return dot_t(coeff[0], right[0, rows, :]) + dot_t(coeff[1], right[1, rows, :])

    @pl.when(jnp.logical_not(info.owner))
    def _():
        for out, rel in zip(outs, rels):
            out[...] = low(rows_of(row_piece(info, rel))).astype(BF16)

    @pl.when(info.owner)
    def _():
        for out, rel in zip(outs, rels):
            piece = row_piece(info, rel)
            rows = rows_of(piece)
            rest = total(dot(y_mate[q], dense[rows_of(2 * q + 1 - info.core), rows]) for q in range(4))
            out[...] = (low(rows) + dense_sum[piece] + rest).astype(BF16)


def call(kernel, name, operands, outs, flops, moved, buckets=None):
    return pl.pallas_call(
        kernel,
        name=name,
        out_shape=outs,
        in_specs=[VMEM] * (len(operands) + (buckets is not None)),
        out_specs=[VMEM] * len(outs),
        compiler_params=pltpu.CompilerParams(vmem_limit_bytes=16 * 2**20),
        cost_estimate=pl.CostEstimate(flops=flops, bytes_accessed=moved, transcendentals=0),
    )(*([] if buckets is None else [buckets]), *operands)


def swap(x, axis, bits):
    size = lax.axis_size(axis)
    return lax.ppermute(x, axis, [(i, i ^ bits) for i in range(size)])


def gather(own, axis, ring, side, first=None):
    got = {(0, 0): own}
    got[(0, 1)] = swap(own, axis, side)
    if first is not None:
        got[(0, 1)], first = lax.optimization_barrier((got[(0, 1)], first))
    got[(2, 0)] = swap(own, axis, 2 * ring)
    got[(1, 0)] = swap(own, axis, ring)
    got[(3, 0)] = swap(own, axis, 3 * ring)
    got[(1, 1)] = swap(got[(0, 1)], axis, ring)
    got[(3, 1)] = swap(got[(0, 1)], axis, 3 * ring)
    got[(2, 1)] = swap(got[(2, 0)], axis, side)
    return [got[rel] for rel in REL], first


def add(*parts):
    return total(v.astype(F32) for v in parts).astype(BF16)


def scatter(pieces, axis, ring, side):
    piece = dict(zip(FAR + NEAR, pieces))
    far_1 = swap(piece[(1, 1)], axis, ring)
    far_3 = swap(piece[(3, 1)], axis, 3 * ring)
    far_2 = swap(piece[(2, 1)], axis, side)
    near_1 = swap(piece[(1, 0)], axis, ring)
    near_3 = swap(piece[(3, 0)], axis, 3 * ring)
    near_2 = swap(add(piece[(2, 0)], far_2), axis, 2 * ring)
    crossed = swap(add(piece[(0, 1)], far_1, far_3), axis, side)
    return add(piece[(0, 0)], near_1, near_3, near_2, crossed)


def body(signal, left_factors, right_factors, dense_diagonal, buckets):
    buckets = buckets.T
    right = right_factors[:, 0]
    left = left_factors[:, 0]
    dense = dense_diagonal[0]
    owners = [((b // 2) * 16 + b, (b // 2) * 16 + (b ^ 1)) for b in range(16)]

    count = signal.shape[0]
    unit = 2 * count * PIECE * PIECE
    size = count * PIECE * 2
    piece = jax.ShapeDtypeStruct((count, PIECE), BF16)
    pair = jax.ShapeDtypeStruct((2, count, PIECE), BF16)
    pair_wide = jax.ShapeDtypeStruct((2, count, PIECE), F32)
    four = jax.ShapeDtypeStruct((4, count, PIECE), BF16)
    eight_wide = jax.ShapeDtypeStruct((8, count, PIECE), F32)

    left_mate = swap(left, "tcol", 1)
    x, left_mate = gather(signal, "trow", 1, 4, left_mate)
    (coeff,) = call(coeff_kernel, "coeff", [*x, right], [pair], 16 * unit, 10 * size + 2**21, buckets)
    coeff_mate = swap(coeff, "tcol", 1)
    (dense_sent,) = call(functools.partial(diag_kernel, 1), "diag_mate", [*x, dense], [four], 32 * unit, 12 * size + 2**23)
    dense_mate = lax.ppermute(dense_sent, ("trow", "tcol"), owners)
    (dense_own,) = call(functools.partial(diag_kernel, 0), "diag_own", [*x, dense], [four], 32 * unit, 12 * size + 2**23)
    terms = []
    for rels in (FAR, NEAR):
        terms += call(
            functools.partial(term_kernel, rels),
            "term",
            [coeff, coeff_mate, left, left_mate, dense_own, dense_mate],
            [piece] * len(rels),
            2 * len(rels) * unit,
            2 * len(rels) * size + 2**21,
        )
    first = scatter(terms, "tcol", 4, 2)
    y, _ = gather(first, "tcol", 4, 2)
    (y_sent,) = call(pack_kernel, "pack", y, [four], 0, 12 * size)
    y_mate = lax.ppermute(y_sent, ("trow", "tcol"), owners)
    own, mate = call(back_kernel, "back", [*y, left, left_mate], [pair_wide, pair], 16 * unit, 14 * size + 2**21)
    mate = swap(mate, "tcol", 1)
    (dense_sum,) = call(diag_back_kernel, "diag_back", [*y, dense], [eight_wide], 32 * unit, 24 * size + 2**22)
    terms = []
    for rels in (FAR, NEAR):
        terms += call(
            functools.partial(second_kernel, rels),
            "second",
            [own, mate, right, dense_sum, y_mate, dense],
            [piece] * len(rels),
            6 * len(rels) * unit,
            4 * len(rels) * size + 3 * 2**20,
            buckets,
        )
    second = scatter(terms, "trow", 1, 4)
    return (first, second)


def solution(mesh):
    in_specs = (
        P(None, ("tcol", "trow")),
        P("trow", "tcol", None, None),
        P("trow", "tcol", None, None),
        P("tcol", None, None),
        P("trow", "tcol"),
    )
    out_specs = (P(None, ("trow", "tcol")), P(None, ("tcol", "trow")))
    return jax.shard_map(body, mesh=mesh, in_specs=in_specs, out_specs=out_specs, check_vma=False)
```

```python
import functools

import jax
import jax.numpy as jnp
from jax import lax
from jax.experimental import pallas as pl
from jax.experimental.pallas import tpu as pltpu
from jax.sharding import PartitionSpec as P

PIECE = 256
F32 = jnp.float32
BF16 = jnp.bfloat16
REL = [(d, x) for d in range(4) for x in range(2)]
FAR = [(1, 1), (3, 1), (2, 1)]
NEAR = [(1, 0), (3, 0), (2, 0), (0, 1), (0, 0)]
VMEM = pl.BlockSpec(memory_space=pltpu.VMEM)


def dot(a, b):
    return lax.dot_general(a, b, (((1,), (0,)), ((), ())), preferred_element_type=F32)


def dot_t(a, b):
    return lax.dot_general(a, b, (((1,), (1,)), ((), ())), preferred_element_type=F32)


def total(parts):
    return functools.reduce(lambda a, b: a + b, parts)


class Place:
    def __init__(self, buckets=None):
        trow = lax.axis_index("trow")
        tcol = lax.axis_index("tcol")
        self.x_lo, self.z = trow >> 2, trow & 3
        self.y, self.x_hi, self.core = tcol >> 2, (tcol >> 1) & 1, tcol & 1
        self.owner = trow == tcol >> 1
        if buckets is not None:
            self.ranks = [jnp.where(trow * 2 + t == tcol, 0, 16 << buckets[:, t : t + 1]) for t in range(2)]


def row_piece(info, rel):
    return (info.x_lo ^ rel[1]) * 4 + (info.z ^ rel[0])


def half_piece(info, rel):
    return (info.y ^ rel[0]) * 2 + (info.x_hi ^ rel[1])


def rows_of(piece):
    return pl.ds(pl.multiple_of(piece * PIECE, PIECE), PIECE)


def left_rows(info, piece):
    return rows_of((piece % 4) * 2 + info.core)


def masked(values, rank):
    columns = lax.broadcasted_iota(jnp.int32, values.shape, 1)
    return jnp.where(columns < rank, values, 0.0)


def coeff_kernel(buckets, *refs):
    info = Place(buckets)
    x, right, out = refs[:8], refs[8], refs[9]
    for t in range(2):
        acc = total(dot(x[n][...], right[t, rows_of(row_piece(info, rel)), :]) for n, rel in enumerate(REL))
        out[t] = masked(acc, info.ranks[t]).astype(BF16)


def diag_kernel(for_mate, *refs):
    info = Place()
    x, dense, out = refs[:8], refs[8], refs[9]
    parity = info.core ^ for_mate

    @pl.when(info.owner)
    def _():
        for q in range(4):
            rows = rows_of(2 * q + parity)
            acc = total(dot_t(x[n][...], dense[rows, rows_of(row_piece(info, rel))]) for n, rel in enumerate(REL))
            out[q] = acc.astype(out.dtype)


def term_kernel(rels, own, mate, left_own, left_mate, dense_own, dense_mate, *outs):
    info = Place()

    def low(piece):
        tile = piece // 4
        rows = left_rows(info, piece)
        return dot_t(own[tile], left_own[tile, rows, :]) + dot_t(mate[tile], left_mate[tile, rows, :])

    @pl.when(jnp.logical_not(info.owner))
    def _():
        for out, rel in zip(outs, rels):
            out[...] = low(half_piece(info, rel)).astype(BF16)

    @pl.when(info.owner)
    def _():
        for out, rel in zip(outs, rels):
            piece = half_piece(info, rel)
            extra = jnp.where(piece // 4 == info.core, dense_own[piece % 4], dense_mate[piece % 4])
            out[...] = (low(piece) + extra.astype(F32)).astype(BF16)


def pack_kernel(*refs):
    info = Place()
    y, out = refs[:8], refs[8]
    for n, rel in enumerate(REL):
        piece = half_piece(info, rel)

        @pl.when(jnp.logical_and(info.owner, piece // 4 != info.core))
        def _():
            out[piece % 4] = y[n][...]


def back_kernel(*refs):
    info = Place()
    y, left_own, left_mate, own, mate = refs[:8], refs[8], refs[9], refs[10], refs[11]
    for half in range(2):
        tile = (info.y // 2) ^ half
        for left, out in ((left_mate, mate), (left_own, own)):
            out[tile] = total(
                dot(y[n][...], left[tile, left_rows(info, half_piece(info, rel)), :])
                for n, rel in enumerate(REL)
                if rel[0] // 2 == half
            ).astype(out.dtype)


def diag_back_kernel(*refs):
    info = Place()
    y, dense, out = refs[:8], refs[8], refs[9]
    for half in range(2):

        @pl.when(jnp.logical_and(info.owner, (info.y // 2) ^ half == info.core))
        def _():
            for p in range(8):
                out[p] = total(
                    dot(y[n][...], dense[left_rows(info, half_piece(info, rel)), p * PIECE : (p + 1) * PIECE])
                    for n, rel in enumerate(REL)
                    if rel[0] // 2 == half
                )


def second_kernel(rels, buckets, own, mate, right, dense_sum, y_mate, dense, *outs):
    info = Place(buckets)
    coeff = [masked(own[t] + mate[t].astype(F32), info.ranks[t]).astype(BF16) for t in range(2)]

    def low(rows):
        return dot_t(coeff[0], right[0, rows, :]) + dot_t(coeff[1], right[1, rows, :])

    @pl.when(jnp.logical_not(info.owner))
    def _():
        for out, rel in zip(outs, rels):
            out[...] = low(rows_of(row_piece(info, rel))).astype(BF16)

    @pl.when(info.owner)
    def _():
        for out, rel in zip(outs, rels):
            piece = row_piece(info, rel)
            rows = rows_of(piece)
            rest = total(dot(y_mate[q], dense[rows_of(2 * q + 1 - info.core), rows]) for q in range(4))
            out[...] = (low(rows) + dense_sum[piece] + rest).astype(BF16)


def load_kernel(right, signal, dense, right_out, signal_out, dense_out, sems):
    copies = [
        pltpu.make_async_copy(right, right_out, sems.at[0]),
        pltpu.make_async_copy(signal, signal_out, sems.at[1]),
    ]
    for copy in copies:
        copy.start()

    @pl.when(Place().owner)
    def _():
        blocks = [pltpu.make_async_copy(dense.at[rows_of(p), :], dense_out.at[rows_of(p), :], sems.at[2 + p]) for p in range(8)]
        for block in blocks:
            block.start()
        for block in blocks:
            block.wait()

    for copy in copies:
        copy.wait()


def load(*arrays):
    return pl.pallas_call(
        load_kernel,
        name="load",
        out_shape=[pltpu.VMEM(v.shape, v.dtype) for v in arrays],
        in_specs=[pl.BlockSpec(memory_space=pltpu.HBM)] * len(arrays),
        out_specs=[VMEM] * len(arrays),
        scratch_shapes=[pltpu.SemaphoreType.DMA((10,))],
        compiler_params=pltpu.CompilerParams(vmem_limit_bytes=16 * 2**20),
        cost_estimate=pl.CostEstimate(flops=0, bytes_accessed=20 * 2**20, transcendentals=0),
    )(*(pltpu.with_memory_space_constraint(v, pltpu.HBM) for v in arrays))


def call(kernel, name, operands, outs, flops, moved, buckets=None):
    return pl.pallas_call(
        kernel,
        name=name,
        out_shape=outs,
        in_specs=[VMEM] * (len(operands) + (buckets is not None)),
        out_specs=[VMEM] * len(outs),
        compiler_params=pltpu.CompilerParams(vmem_limit_bytes=16 * 2**20),
        cost_estimate=pl.CostEstimate(flops=flops, bytes_accessed=moved, transcendentals=0),
    )(*([] if buckets is None else [buckets]), *operands)


def swap(x, axis, bits):
    size = lax.axis_size(axis)
    return lax.ppermute(x, axis, [(i, i ^ bits) for i in range(size)])


def gather(own, axis, ring, side, first=None, loaded=()):
    got = {(0, 0): own}
    got[(0, 1)] = swap(own, axis, side)
    if first is not None:
        got[(0, 1)], first = lax.optimization_barrier((got[(0, 1)], first))
    got[(2, 0)] = swap(own, axis, 2 * ring)
    if first is not None:
        got[(2, 0)], *loaded = lax.optimization_barrier((got[(2, 0)], *loaded))
    got[(1, 0)] = swap(own, axis, ring)
    got[(3, 0)] = swap(own, axis, 3 * ring)
    got[(1, 1)] = swap(got[(0, 1)], axis, ring)
    got[(3, 1)] = swap(got[(0, 1)], axis, 3 * ring)
    got[(2, 1)] = swap(got[(2, 0)], axis, side)
    return [got[rel] for rel in REL], first, loaded


def add(*parts):
    return total(v.astype(F32) for v in parts).astype(BF16)


def scatter(pieces, axis, ring, side):
    piece = dict(zip(FAR + NEAR, pieces))
    far_1 = swap(piece[(1, 1)], axis, ring)
    far_3 = swap(piece[(3, 1)], axis, 3 * ring)
    far_2 = swap(piece[(2, 1)], axis, side)
    near_1 = swap(piece[(1, 0)], axis, ring)
    near_3 = swap(piece[(3, 0)], axis, 3 * ring)
    near_2 = swap(add(piece[(2, 0)], far_2), axis, 2 * ring)
    crossed = swap(add(piece[(0, 1)], far_1, far_3), axis, side)
    return add(piece[(0, 0)], near_1, near_3, near_2, crossed)


def body(signal, left_factors, right_factors, dense_diagonal, buckets):
    buckets = buckets.T
    right = right_factors[:, 0]
    left = left_factors[:, 0]
    dense = dense_diagonal[0]
    owners = [((b // 2) * 16 + b, (b // 2) * 16 + (b ^ 1)) for b in range(16)]

    count = signal.shape[0]
    unit = 2 * count * PIECE * PIECE
    size = count * PIECE * 2
    piece = jax.ShapeDtypeStruct((count, PIECE), BF16)
    pair = jax.ShapeDtypeStruct((2, count, PIECE), BF16)
    pair_wide = jax.ShapeDtypeStruct((2, count, PIECE), F32)
    four = jax.ShapeDtypeStruct((4, count, PIECE), BF16)
    eight_wide = jax.ShapeDtypeStruct((8, count, PIECE), F32)

    left_mate = swap(left, "tcol", 1)
    x, left_mate, loaded = gather(signal, "trow", 1, 4, left_mate, load(right, signal, dense))
    right, x[0], dense = loaded
    (coeff,) = call(coeff_kernel, "coeff", [*x, right], [pair], 16 * unit, 10 * size + 2**21, buckets)
    coeff_mate = swap(coeff, "tcol", 1)
    (dense_sent,) = call(functools.partial(diag_kernel, 1), "diag_mate", [*x, dense], [four], 32 * unit, 12 * size + 2**23)
    dense_mate = lax.ppermute(dense_sent, ("trow", "tcol"), owners)
    (dense_own,) = call(functools.partial(diag_kernel, 0), "diag_own", [*x, dense], [four], 32 * unit, 12 * size + 2**23)
    terms = []
    for rels in (FAR, NEAR):
        terms += call(
            functools.partial(term_kernel, rels),
            "term",
            [coeff, coeff_mate, left, left_mate, dense_own, dense_mate],
            [piece] * len(rels),
            2 * len(rels) * unit,
            2 * len(rels) * size + 2**21,
        )
    first = scatter(terms, "tcol", 4, 2)
    y, _, _ = gather(first, "tcol", 4, 2)
    (y_sent,) = call(pack_kernel, "pack", y, [four], 0, 12 * size)
    y_mate = lax.ppermute(y_sent, ("trow", "tcol"), owners)
    own, mate = call(back_kernel, "back", [*y, left, left_mate], [pair_wide, pair], 16 * unit, 14 * size + 2**21)
    mate = swap(mate, "tcol", 1)
    (dense_sum,) = call(diag_back_kernel, "diag_back", [*y, dense], [eight_wide], 32 * unit, 24 * size + 2**22)
    terms = []
    for rels in (FAR, NEAR):
        terms += call(
            functools.partial(second_kernel, rels),
            "second",
            [own, mate, right, dense_sum, y_mate, dense],
            [piece] * len(rels),
            6 * len(rels) * unit,
            4 * len(rels) * size + 3 * 2**20,
            buckets,
        )
    second = scatter(terms, "trow", 1, 4)
    return (first, second)


def solution(mesh):
    in_specs = (
        P(None, ("tcol", "trow")),
        P("trow", "tcol", None, None),
        P("trow", "tcol", None, None),
        P("tcol", None, None),
        P("trow", "tcol"),
    )
    out_specs = (P(None, ("trow", "tcol")), P(None, ("tcol", "trow")))
    return jax.shard_map(body, mesh=mesh, in_specs=in_specs, out_specs=out_specs, check_vma=False)
```

```python
import functools

import jax
import jax.numpy as jnp
from jax import lax
from jax.experimental import pallas as pl
from jax.experimental.pallas import tpu as pltpu
from jax.sharding import PartitionSpec as P

PIECE = 256
F32 = jnp.float32
BF16 = jnp.bfloat16
REL = [(d, x) for d in range(4) for x in range(2)]
FAR = [(1, 1), (3, 1), (2, 1)]
NEAR = [(1, 0), (3, 0), (2, 0), (0, 1), (0, 0)]
VMEM = pl.BlockSpec(memory_space=pltpu.VMEM)


def dot(a, b):
    return lax.dot_general(a, b, (((1,), (0,)), ((), ())), preferred_element_type=F32)


def dot_t(a, b):
    return lax.dot_general(a, b, (((1,), (1,)), ((), ())), preferred_element_type=F32)


def total(parts):
    return functools.reduce(lambda a, b: a + b, parts)


class Place:
    def __init__(self, buckets=None):
        trow = lax.axis_index("trow")
        tcol = lax.axis_index("tcol")
        self.x_lo, self.z = trow >> 2, trow & 3
        self.y, self.x_hi, self.core = tcol >> 2, (tcol >> 1) & 1, tcol & 1
        self.owner = trow == tcol >> 1
        if buckets is not None:
            self.ranks = [jnp.where(trow * 2 + t == tcol, 0, 16 << buckets[:, t : t + 1]) for t in range(2)]


def row_piece(info, rel):
    return (info.x_lo ^ rel[1]) * 4 + (info.z ^ rel[0])


def half_piece(info, rel):
    return (info.y ^ rel[0]) * 2 + (info.x_hi ^ rel[1])


def rows_of(piece):
    return pl.ds(pl.multiple_of(piece * PIECE, PIECE), PIECE)


def left_rows(info, piece):
    return rows_of((piece % 4) * 2 + info.core)


def masked(values, rank):
    columns = lax.broadcasted_iota(jnp.int32, values.shape, 1)
    return jnp.where(columns < rank, values, 0.0)


def coeff_kernel(buckets, *refs):
    info = Place(buckets)
    x, right, out = refs[:8], refs[8], refs[9]
    for t in range(2):
        acc = total(dot(x[n][...], right[t, rows_of(row_piece(info, rel)), :]) for n, rel in enumerate(REL))
        out[t] = masked(acc, info.ranks[t]).astype(BF16)


def diag_kernel(for_mate, *refs):
    info = Place()
    x, dense, out = refs[:8], refs[8], refs[9]
    parity = info.core ^ for_mate

    @pl.when(info.owner)
    def _():
        for q in range(4):
            rows = rows_of(2 * q + parity)
            acc = total(dot_t(x[n][...], dense[rows, rows_of(row_piece(info, rel))]) for n, rel in enumerate(REL))
            out[q] = acc.astype(out.dtype)


def term_kernel(rels, own, mate, left_own, left_mate, dense_own, dense_mate, *outs):
    info = Place()

    def low(piece):
        tile = piece // 4
        rows = left_rows(info, piece)
        return dot_t(own[tile], left_own[tile, rows, :]) + dot_t(mate[tile], left_mate[tile, rows, :])

    @pl.when(jnp.logical_not(info.owner))
    def _():
        for out, rel in zip(outs, rels):
            out[...] = low(half_piece(info, rel)).astype(BF16)

    @pl.when(info.owner)
    def _():
        for out, rel in zip(outs, rels):
            piece = half_piece(info, rel)
            extra = jnp.where(piece // 4 == info.core, dense_own[piece % 4], dense_mate[piece % 4])
            out[...] = (low(piece) + extra.astype(F32)).astype(BF16)


def pack_kernel(*refs):
    info = Place()
    y, out = refs[:8], refs[8]
    for n, rel in enumerate(REL):
        piece = half_piece(info, rel)

        @pl.when(jnp.logical_and(info.owner, piece // 4 != info.core))
        def _():
            out[piece % 4] = y[n][...]


def back_kernel(*refs):
    info = Place()
    y, left_own, left_mate, own, mate = refs[:8], refs[8], refs[9], refs[10], refs[11]
    for half in range(2):
        tile = (info.y // 2) ^ half
        for left, out in ((left_mate, mate), (left_own, own)):
            out[tile] = total(
                dot(y[n][...], left[tile, left_rows(info, half_piece(info, rel)), :])
                for n, rel in enumerate(REL)
                if rel[0] // 2 == half
            ).astype(out.dtype)


def diag_back_kernel(*refs):
    info = Place()
    y, dense, out = refs[:8], refs[8], refs[9]
    for half in range(2):

        @pl.when(jnp.logical_and(info.owner, (info.y // 2) ^ half == info.core))
        def _():
            for p in range(8):
                out[p] = total(
                    dot(y[n][...], dense[left_rows(info, half_piece(info, rel)), p * PIECE : (p + 1) * PIECE])
                    for n, rel in enumerate(REL)
                    if rel[0] // 2 == half
                )


def second_kernel(rels, buckets, own, mate, right, dense_sum, y_mate, dense, *outs):
    info = Place(buckets)
    coeff = [masked(own[t] + mate[t].astype(F32), info.ranks[t]).astype(BF16) for t in range(2)]

    def low(rows):
        return dot_t(coeff[0], right[0, rows, :]) + dot_t(coeff[1], right[1, rows, :])

    @pl.when(jnp.logical_not(info.owner))
    def _():
        for out, rel in zip(outs, rels):
            out[...] = low(rows_of(row_piece(info, rel))).astype(BF16)

    @pl.when(info.owner)
    def _():
        for out, rel in zip(outs, rels):
            piece = row_piece(info, rel)
            rows = rows_of(piece)
            rest = total(dot(y_mate[q], dense[rows_of(2 * q + 1 - info.core), rows]) for q in range(4))
            out[...] = (low(rows) + dense_sum[piece] + rest).astype(BF16)


def load_kernel(right, signal, dense, right_out, signal_out, dense_out, sems):
    copies = [
        pltpu.make_async_copy(right, right_out, sems.at[0]),
        pltpu.make_async_copy(signal, signal_out, sems.at[1]),
    ]
    for copy in copies:
        copy.start()

    @pl.when(Place().owner)
    def _():
        blocks = [pltpu.make_async_copy(dense.at[rows_of(p), :], dense_out.at[rows_of(p), :], sems.at[2 + p]) for p in range(8)]
        for block in blocks:
            block.start()
        for block in blocks:
            block.wait()

    for copy in copies:
        copy.wait()


def load(*arrays):
    return pl.pallas_call(
        load_kernel,
        name="load",
        out_shape=[pltpu.VMEM(v.shape, v.dtype) for v in arrays],
        in_specs=[pl.BlockSpec(memory_space=pltpu.HBM)] * len(arrays),
        out_specs=[VMEM] * len(arrays),
        scratch_shapes=[pltpu.SemaphoreType.DMA((10,))],
        compiler_params=pltpu.CompilerParams(vmem_limit_bytes=16 * 2**20),
        cost_estimate=pl.CostEstimate(flops=0, bytes_accessed=20 * 2**20, transcendentals=0),
    )(*(pltpu.with_memory_space_constraint(v, pltpu.HBM) for v in arrays))


def call(kernel, name, operands, outs, flops, moved, buckets=None):
    return pl.pallas_call(
        kernel,
        name=name,
        out_shape=outs,
        in_specs=[VMEM] * (len(operands) + (buckets is not None)),
        out_specs=[VMEM] * len(outs),
        compiler_params=pltpu.CompilerParams(vmem_limit_bytes=16 * 2**20),
        cost_estimate=pl.CostEstimate(flops=flops, bytes_accessed=moved, transcendentals=0),
    )(*([] if buckets is None else [buckets]), *operands)


def swap(x, axis, bits):
    size = lax.axis_size(axis)
    return lax.ppermute(x, axis, [(i, i ^ bits) for i in range(size)])


def gather(own, axis, ring, side, first=None, loaded=()):
    got = {(0, 0): own}
    got[(0, 1)] = swap(own, axis, side)
    if first is not None:
        got[(0, 1)], first = lax.optimization_barrier((got[(0, 1)], first))
    got[(2, 0)] = swap(own, axis, 2 * ring)
    if first is not None:
        got[(2, 0)], *loaded = lax.optimization_barrier((got[(2, 0)], *loaded))
    got[(1, 0)] = swap(own, axis, ring)
    got[(3, 0)] = swap(own, axis, 3 * ring)
    got[(1, 1)] = swap(got[(0, 1)], axis, ring)
    got[(3, 1)] = swap(got[(0, 1)], axis, 3 * ring)
    got[(2, 1)] = swap(got[(2, 0)], axis, side)
    return [got[rel] for rel in REL], first, loaded


def add(*parts):
    return total(v.astype(F32) for v in parts).astype(BF16)


def scatter(pieces, axis, ring, side):
    piece = dict(zip(FAR + NEAR, pieces))
    far_1 = swap(piece[(1, 1)], axis, ring)
    far_3 = swap(piece[(3, 1)], axis, 3 * ring)
    far_2 = swap(piece[(2, 1)], axis, side)
    near_1 = swap(piece[(1, 0)], axis, ring)
    near_3 = swap(piece[(3, 0)], axis, 3 * ring)
    near_2 = swap(add(piece[(2, 0)], far_2), axis, 2 * ring)
    crossed = swap(add(piece[(0, 1)], far_1, far_3), axis, side)
    return add(piece[(0, 0)], near_1, near_3, near_2, crossed)


def body(signal, left_factors, right_factors, dense_diagonal, buckets):
    buckets = buckets.T
    right = right_factors[:, 0]
    left = left_factors[:, 0]
    dense = dense_diagonal[0]

    count = signal.shape[0]
    unit = 2 * count * PIECE * PIECE
    size = count * PIECE * 2
    piece = jax.ShapeDtypeStruct((count, PIECE), BF16)
    pair = jax.ShapeDtypeStruct((2, count, PIECE), BF16)
    pair_wide = jax.ShapeDtypeStruct((2, count, PIECE), F32)
    four = jax.ShapeDtypeStruct((4, count, PIECE), BF16)
    eight_wide = jax.ShapeDtypeStruct((8, count, PIECE), F32)

    left_mate = swap(left, "tcol", 1)
    x, left_mate, loaded = gather(signal, "trow", 1, 4, left_mate, load(right, signal, dense))
    right, x[0], dense = loaded
    (coeff,) = call(coeff_kernel, "coeff", [*x, right], [pair], 16 * unit, 10 * size + 2**21, buckets)
    coeff_mate = swap(coeff, "tcol", 1)
    (dense_sent,) = call(functools.partial(diag_kernel, 1), "diag_mate", [*x, dense], [four], 32 * unit, 12 * size + 2**23)
    dense_mate = swap(dense_sent, "tcol", 1)
    (dense_own,) = call(functools.partial(diag_kernel, 0), "diag_own", [*x, dense], [four], 32 * unit, 12 * size + 2**23)
    terms = []
    for rels in (FAR, NEAR):
        terms += call(
            functools.partial(term_kernel, rels),
            "term",
            [coeff, coeff_mate, left, left_mate, dense_own, dense_mate],
            [piece] * len(rels),
            2 * len(rels) * unit,
            2 * len(rels) * size + 2**21,
        )
    first = scatter(terms, "tcol", 4, 2)
    y, _, _ = gather(first, "tcol", 4, 2)
    (y_sent,) = call(pack_kernel, "pack", y, [four], 0, 12 * size)
    y_mate = swap(y_sent, "tcol", 1)
    own, mate = call(back_kernel, "back", [*y, left, left_mate], [pair_wide, pair], 16 * unit, 14 * size + 2**21)
    mate = swap(mate, "tcol", 1)
    (dense_sum,) = call(diag_back_kernel, "diag_back", [*y, dense], [eight_wide], 32 * unit, 24 * size + 2**22)
    terms = []
    for rels in (FAR, NEAR):
        terms += call(
            functools.partial(second_kernel, rels),
            "second",
            [own, mate, right, dense_sum, y_mate, dense],
            [piece] * len(rels),
            6 * len(rels) * unit,
            4 * len(rels) * size + 3 * 2**20,
            buckets,
        )
    second = scatter(terms, "trow", 1, 4)
    return (first, second)


def solution(mesh):
    in_specs = (
        P(None, ("tcol", "trow")),
        P("trow", "tcol", None, None),
        P("trow", "tcol", None, None),
        P("tcol", None, None),
        P("trow", "tcol"),
    )
    out_specs = (P(None, ("trow", "tcol")), P(None, ("tcol", "trow")))
    return jax.shard_map(body, mesh=mesh, in_specs=in_specs, out_specs=out_specs, check_vma=False)
```

```python
import functools

import jax
import jax.numpy as jnp
from jax import lax
from jax.experimental import pallas as pl
from jax.experimental.pallas import tpu as pltpu
from jax.sharding import PartitionSpec as P

PIECE = 256
F32 = jnp.float32
BF16 = jnp.bfloat16
REL = [(d, x) for d in range(4) for x in range(2)]
FAR = [(1, 1), (3, 1), (2, 1)]
NEAR = [(1, 0), (3, 0), (2, 0), (0, 1), (0, 0)]
VMEM = pl.BlockSpec(memory_space=pltpu.VMEM)


def dot(a, b):
    return lax.dot_general(a, b, (((1,), (0,)), ((), ())), preferred_element_type=F32)


def dot_t(a, b):
    return lax.dot_general(a, b, (((1,), (1,)), ((), ())), preferred_element_type=F32)


def total(parts):
    return functools.reduce(lambda a, b: a + b, parts)


class Place:
    def __init__(self, buckets=None):
        trow = lax.axis_index("trow")
        tcol = lax.axis_index("tcol")
        self.x_lo, self.z = trow >> 2, trow & 3
        self.y, self.x_hi, self.core = tcol >> 2, (tcol >> 1) & 1, tcol & 1
        self.owner = trow == tcol >> 1
        if buckets is not None:
            self.ranks = [jnp.where(trow * 2 + t == tcol, 0, 16 << buckets[:, t : t + 1]) for t in range(2)]


def row_piece(info, rel):
    return (info.x_lo ^ rel[1]) * 4 + (info.z ^ rel[0])


def half_piece(info, rel):
    return (info.y ^ rel[0]) * 2 + (info.x_hi ^ rel[1])


def rows_of(piece):
    return pl.ds(pl.multiple_of(piece * PIECE, PIECE), PIECE)


def left_rows(info, piece):
    return rows_of((piece % 4) * 2 + info.core)


def masked(values, rank):
    columns = lax.broadcasted_iota(jnp.int32, values.shape, 1)
    return jnp.where(columns < rank, values, 0.0)


def coeff_kernel(buckets, *refs):
    info = Place(buckets)
    x, right, out = refs[:8], refs[8], refs[9]
    for t in range(2):
        acc = total(dot(x[n][...], right[t, rows_of(row_piece(info, rel)), :]) for n, rel in enumerate(REL))
        out[t] = masked(acc, info.ranks[t]).astype(BF16)


def diag_kernel(for_mate, *refs):
    info = Place()
    x, dense, out = refs[:8], refs[8], refs[9]
    parity = info.core ^ for_mate

    @pl.when(info.owner)
    def _():
        for q in range(4):
            rows = rows_of(2 * q + parity)
            acc = total(dot_t(x[n][...], dense[rows, rows_of(row_piece(info, rel))]) for n, rel in enumerate(REL))
            out[q] = acc.astype(out.dtype)


def term_kernel(rels, own, mate, left_own, left_mate, dense_own, dense_mate, *outs):
    info = Place()

    def low(piece):
        tile = piece // 4
        rows = left_rows(info, piece)
        return dot_t(own[tile], left_own[tile, rows, :]) + dot_t(mate[tile], left_mate[tile, rows, :])

    @pl.when(jnp.logical_not(info.owner))
    def _():
        for out, rel in zip(outs, rels):
            out[...] = low(half_piece(info, rel)).astype(BF16)

    @pl.when(info.owner)
    def _():
        for out, rel in zip(outs, rels):
            piece = half_piece(info, rel)
            extra = jnp.where(piece // 4 == info.core, dense_own[piece % 4], dense_mate[piece % 4])
            out[...] = (low(piece) + extra.astype(F32)).astype(BF16)


def pack_kernel(*refs):
    info = Place()
    y, out = refs[:8], refs[8]
    for n, rel in enumerate(REL):
        piece = half_piece(info, rel)

        @pl.when(jnp.logical_and(info.owner, piece // 4 != info.core))
        def _():
            out[piece % 4] = y[n][...]


def back_kernel(*refs):
    info = Place()
    y, left_own, left_mate, own, mate = refs[:8], refs[8], refs[9], refs[10], refs[11]
    for half in range(2):
        tile = (info.y // 2) ^ half
        for left, out in ((left_mate, mate), (left_own, own)):
            out[tile] = total(
                dot(y[n][...], left[tile, left_rows(info, half_piece(info, rel)), :])
                for n, rel in enumerate(REL)
                if rel[0] // 2 == half
            ).astype(out.dtype)


def diag_back_kernel(*refs):
    info = Place()
    y, dense, out = refs[:8], refs[8], refs[9]
    for half in range(2):

        @pl.when(jnp.logical_and(info.owner, (info.y // 2) ^ half == info.core))
        def _():
            for p in range(8):
                out[p] = total(
                    dot(y[n][...], dense[left_rows(info, half_piece(info, rel)), p * PIECE : (p + 1) * PIECE])
                    for n, rel in enumerate(REL)
                    if rel[0] // 2 == half
                )


def second_kernel(rels, buckets, own, mate, right, dense_sum, y_mate, dense, *outs):
    info = Place(buckets)
    coeff = [masked(own[t] + mate[t].astype(F32), info.ranks[t]).astype(BF16) for t in range(2)]

    def low(rows):
        return dot_t(coeff[0], right[0, rows, :]) + dot_t(coeff[1], right[1, rows, :])

    @pl.when(jnp.logical_not(info.owner))
    def _():
        for out, rel in zip(outs, rels):
            out[...] = low(rows_of(row_piece(info, rel))).astype(BF16)

    @pl.when(info.owner)
    def _():
        for out, rel in zip(outs, rels):
            piece = row_piece(info, rel)
            rows = rows_of(piece)
            rest = total(dot(y_mate[q], dense[rows_of(2 * q + 1 - info.core), rows]) for q in range(4))
            out[...] = (low(rows) + dense_sum[piece] + rest).astype(BF16)


def load_kernel(dense, dense_out, sems):
    @pl.when(Place().owner)
    def _():
        blocks = [pltpu.make_async_copy(dense.at[rows_of(p), :], dense_out.at[rows_of(p), :], sems.at[p]) for p in range(8)]
        for block in blocks:
            block.start()
        for block in blocks:
            block.wait()


def load(*arrays):
    return pl.pallas_call(
        load_kernel,
        name="load",
        out_shape=[pltpu.VMEM(v.shape, v.dtype) for v in arrays],
        in_specs=[pl.BlockSpec(memory_space=pltpu.HBM)] * len(arrays),
        out_specs=[VMEM] * len(arrays),
        scratch_shapes=[pltpu.SemaphoreType.DMA((10,))],
        compiler_params=pltpu.CompilerParams(vmem_limit_bytes=16 * 2**20),
        cost_estimate=pl.CostEstimate(flops=0, bytes_accessed=20 * 2**20, transcendentals=0),
    )(*(pltpu.with_memory_space_constraint(v, pltpu.HBM) for v in arrays))


def call(kernel, name, operands, outs, flops, moved, buckets=None):
    return pl.pallas_call(
        kernel,
        name=name,
        out_shape=outs,
        in_specs=[VMEM] * (len(operands) + (buckets is not None)),
        out_specs=[VMEM] * len(outs),
        compiler_params=pltpu.CompilerParams(vmem_limit_bytes=16 * 2**20),
        cost_estimate=pl.CostEstimate(flops=flops, bytes_accessed=moved, transcendentals=0),
    )(*([] if buckets is None else [buckets]), *operands)


def swap(x, axis, bits):
    size = lax.axis_size(axis)
    return lax.ppermute(x, axis, [(i, i ^ bits) for i in range(size)])


def gather(own, axis, ring, side, first=None, loaded=()):
    got = {(0, 0): own}
    got[(0, 1)] = swap(own, axis, side)
    got[(2, 0)] = swap(own, axis, 2 * ring)
    if first is not None:
        got[(2, 0)], first, *loaded = lax.optimization_barrier((got[(2, 0)], first, *loaded))
    got[(1, 0)] = swap(own, axis, ring)
    got[(3, 0)] = swap(own, axis, 3 * ring)
    got[(1, 1)] = swap(got[(0, 1)], axis, ring)
    got[(3, 1)] = swap(got[(0, 1)], axis, 3 * ring)
    got[(2, 1)] = swap(got[(2, 0)], axis, side)
    return [got[rel] for rel in REL], first, loaded


def add(*parts):
    return total(v.astype(F32) for v in parts).astype(BF16)


def scatter(pieces, axis, ring, side):
    piece = dict(zip(FAR + NEAR, pieces))
    far_1 = swap(piece[(1, 1)], axis, ring)
    far_3 = swap(piece[(3, 1)], axis, 3 * ring)
    far_2 = swap(piece[(2, 1)], axis, side)
    near_1 = swap(piece[(1, 0)], axis, ring)
    near_3 = swap(piece[(3, 0)], axis, 3 * ring)
    near_2 = swap(add(piece[(2, 0)], far_2), axis, 2 * ring)
    crossed = swap(add(piece[(0, 1)], far_1, far_3), axis, side)
    return add(piece[(0, 0)], near_1, near_3, near_2, crossed)


def body(signal, left_factors, right_factors, dense_diagonal, buckets):
    buckets = buckets.T
    right = right_factors[:, 0]
    left = left_factors[:, 0]
    dense = dense_diagonal[0]

    count = signal.shape[0]
    unit = 2 * count * PIECE * PIECE
    size = count * PIECE * 2
    piece = jax.ShapeDtypeStruct((count, PIECE), BF16)
    pair = jax.ShapeDtypeStruct((2, count, PIECE), BF16)
    pair_wide = jax.ShapeDtypeStruct((2, count, PIECE), F32)
    four = jax.ShapeDtypeStruct((4, count, PIECE), BF16)
    eight_wide = jax.ShapeDtypeStruct((8, count, PIECE), F32)

    left_mate = swap(left, "tcol", 1)
    x, left_mate, loaded = gather(signal, "trow", 1, 4, left_mate, load(dense))
    (dense,) = loaded
    (coeff,) = call(coeff_kernel, "coeff", [*x, right], [pair], 16 * unit, 10 * size + 2**21, buckets)
    coeff_mate = swap(coeff, "tcol", 1)
    (dense_sent,) = call(functools.partial(diag_kernel, 1), "diag_mate", [*x, dense], [four], 32 * unit, 12 * size + 2**23)
    dense_mate = swap(dense_sent, "tcol", 1)
    (dense_own,) = call(functools.partial(diag_kernel, 0), "diag_own", [*x, dense], [four], 32 * unit, 12 * size + 2**23)
    terms = []
    for rels in (FAR, NEAR):
        terms += call(
            functools.partial(term_kernel, rels),
            "term",
            [coeff, coeff_mate, left, left_mate, dense_own, dense_mate],
            [piece] * len(rels),
            2 * len(rels) * unit,
            2 * len(rels) * size + 2**21,
        )
    first = scatter(terms, "tcol", 4, 2)
    y, _, _ = gather(first, "tcol", 4, 2)
    (y_sent,) = call(pack_kernel, "pack", y, [four], 0, 12 * size)
    y_mate = swap(y_sent, "tcol", 1)
    own, mate = call(back_kernel, "back", [*y, left, left_mate], [pair_wide, pair], 16 * unit, 14 * size + 2**21)
    mate = swap(mate, "tcol", 1)
    (dense_sum,) = call(diag_back_kernel, "diag_back", [*y, dense], [eight_wide], 32 * unit, 24 * size + 2**22)
    terms = []
    for rels in (FAR, NEAR):
        terms += call(
            functools.partial(second_kernel, rels),
            "second",
            [own, mate, right, dense_sum, y_mate, dense],
            [piece] * len(rels),
            6 * len(rels) * unit,
            4 * len(rels) * size + 3 * 2**20,
            buckets,
        )
    second = scatter(terms, "trow", 1, 4)
    return (first, second)


def solution(mesh):
    in_specs = (
        P(None, ("tcol", "trow")),
        P("trow", "tcol", None, None),
        P("trow", "tcol", None, None),
        P("tcol", None, None),
        P("trow", "tcol"),
    )
    out_specs = (P(None, ("trow", "tcol")), P(None, ("tcol", "trow")))
    return jax.shard_map(body, mesh=mesh, in_specs=in_specs, out_specs=out_specs, check_vma=False)
```

```python
import functools

import jax
import jax.numpy as jnp
from jax import lax
from jax.experimental import pallas as pl
from jax.experimental.pallas import tpu as pltpu
from jax.sharding import PartitionSpec as P

PIECE = 256
F32 = jnp.float32
BF16 = jnp.bfloat16
REL = [(d, x) for d in range(4) for x in range(2)]
FAR = [(1, 1), (3, 1), (2, 1)]
NEAR = [(1, 0), (3, 0), (2, 0), (0, 1), (0, 0)]
GROUPS_D = [[(1, 1), (3, 1), (2, 1)], [(2, 0), (0, 1)], [(1, 0), (3, 0), (0, 0)]]
VMEM = pl.BlockSpec(memory_space=pltpu.VMEM)


def dot(a, b):
    return lax.dot_general(a, b, (((1,), (0,)), ((), ())), preferred_element_type=F32)


def dot_t(a, b):
    return lax.dot_general(a, b, (((1,), (1,)), ((), ())), preferred_element_type=F32)


def total(parts):
    return functools.reduce(lambda a, b: a + b, parts)


class Place:
    def __init__(self, buckets=None):
        trow = lax.axis_index("trow")
        tcol = lax.axis_index("tcol")
        self.x_lo, self.z = trow >> 2, trow & 3
        self.y, self.x_hi, self.core = tcol >> 2, (tcol >> 1) & 1, tcol & 1
        self.owner = trow == tcol >> 1
        if buckets is not None:
            self.ranks = [jnp.where(trow * 2 + t == tcol, 0, 16 << buckets[:, t : t + 1]) for t in range(2)]


def row_piece(info, rel):
    return (info.x_lo ^ rel[1]) * 4 + (info.z ^ rel[0])


def half_piece(info, rel):
    return (info.y ^ rel[0]) * 2 + (info.x_hi ^ rel[1])


def rows_of(piece):
    return pl.ds(pl.multiple_of(piece * PIECE, PIECE), PIECE)


def left_rows(info, piece):
    return rows_of((piece % 4) * 2 + info.core)


def masked(values, rank):
    columns = lax.broadcasted_iota(jnp.int32, values.shape, 1)
    return jnp.where(columns < rank, values, 0.0)


def coeff_kernel(buckets, *refs):
    info = Place(buckets)
    x, right, out = refs[:8], refs[8], refs[9]
    for t in range(2):
        acc = total(dot(x[n][...], right[t, rows_of(row_piece(info, rel)), :]) for n, rel in enumerate(REL))
        out[t] = masked(acc, info.ranks[t]).astype(BF16)


def diag_kernel(for_mate, *refs):
    info = Place()
    x, dense, out = refs[:8], refs[8], refs[9]
    parity = info.core ^ for_mate

    @pl.when(info.owner)
    def _():
        for q in range(4):
            rows = rows_of(2 * q + parity)
            acc = total(dot_t(x[n][...], dense[rows, rows_of(row_piece(info, rel))]) for n, rel in enumerate(REL))
            out[q] = acc.astype(out.dtype)


def term_kernel(rels, own, mate, left_own, left_mate, dense_own, dense_mate, *outs):
    info = Place()

    def low(piece):
        tile = piece // 4
        rows = left_rows(info, piece)
        return dot_t(own[tile], left_own[tile, rows, :]) + dot_t(mate[tile], left_mate[tile, rows, :])

    @pl.when(jnp.logical_not(info.owner))
    def _():
        for out, rel in zip(outs, rels):
            out[...] = low(half_piece(info, rel)).astype(BF16)

    @pl.when(info.owner)
    def _():
        for out, rel in zip(outs, rels):
            piece = half_piece(info, rel)
            extra = jnp.where(piece // 4 == info.core, dense_own[piece % 4], dense_mate[piece % 4])
            out[...] = (low(piece) + extra.astype(F32)).astype(BF16)


def pack_kernel(*refs):
    info = Place()
    y, out = refs[:8], refs[8]
    for n, rel in enumerate(REL):
        piece = half_piece(info, rel)

        @pl.when(jnp.logical_and(info.owner, piece // 4 != info.core))
        def _():
            out[piece % 4] = y[n][...]


def back_kernel(*refs):
    info = Place()
    y, left_own, left_mate, own, mate = refs[:8], refs[8], refs[9], refs[10], refs[11]
    for half in range(2):
        tile = (info.y // 2) ^ half
        for left, out in ((left_mate, mate), (left_own, own)):
            out[tile] = total(
                dot(y[n][...], left[tile, left_rows(info, half_piece(info, rel)), :])
                for n, rel in enumerate(REL)
                if rel[0] // 2 == half
            ).astype(out.dtype)


def diag_back_kernel(*refs):
    info = Place()
    y, dense, out = refs[:8], refs[8], refs[9]
    for half in range(2):

        @pl.when(jnp.logical_and(info.owner, (info.y // 2) ^ half == info.core))
        def _():
            for p in range(8):
                out[p] = total(
                    dot(y[n][...], dense[left_rows(info, half_piece(info, rel)), p * PIECE : (p + 1) * PIECE])
                    for n, rel in enumerate(REL)
                    if rel[0] // 2 == half
                )


def second_kernel(rels, buckets, own, mate, right, dense_sum, y_mate, dense, *outs):
    info = Place(buckets)
    coeff = [masked(own[t] + mate[t].astype(F32), info.ranks[t]).astype(BF16) for t in range(2)]

    def low(rows):
        return dot_t(coeff[0], right[0, rows, :]) + dot_t(coeff[1], right[1, rows, :])

    @pl.when(jnp.logical_not(info.owner))
    def _():
        for out, rel in zip(outs, rels):
            out[...] = low(rows_of(row_piece(info, rel))).astype(BF16)

    @pl.when(info.owner)
    def _():
        for out, rel in zip(outs, rels):
            piece = row_piece(info, rel)
            rows = rows_of(piece)
            rest = total(dot(y_mate[q], dense[rows_of(2 * q + 1 - info.core), rows]) for q in range(4))
            out[...] = (low(rows) + dense_sum[piece] + rest).astype(BF16)


def load_kernel(dense, dense_out, sems):
    @pl.when(Place().owner)
    def _():
        blocks = [pltpu.make_async_copy(dense.at[rows_of(p), :], dense_out.at[rows_of(p), :], sems.at[p]) for p in range(8)]
        for block in blocks:
            block.start()
        for block in blocks:
            block.wait()


def load(*arrays):
    return pl.pallas_call(
        load_kernel,
        name="load",
        out_shape=[pltpu.VMEM(v.shape, v.dtype) for v in arrays],
        in_specs=[pl.BlockSpec(memory_space=pltpu.HBM)] * len(arrays),
        out_specs=[VMEM] * len(arrays),
        scratch_shapes=[pltpu.SemaphoreType.DMA((10,))],
        compiler_params=pltpu.CompilerParams(vmem_limit_bytes=16 * 2**20),
        cost_estimate=pl.CostEstimate(flops=0, bytes_accessed=20 * 2**20, transcendentals=0),
    )(*(pltpu.with_memory_space_constraint(v, pltpu.HBM) for v in arrays))


def call(kernel, name, operands, outs, flops, moved, buckets=None):
    return pl.pallas_call(
        kernel,
        name=name,
        out_shape=outs,
        in_specs=[VMEM] * (len(operands) + (buckets is not None)),
        out_specs=[VMEM] * len(outs),
        compiler_params=pltpu.CompilerParams(vmem_limit_bytes=16 * 2**20),
        cost_estimate=pl.CostEstimate(flops=flops, bytes_accessed=moved, transcendentals=0),
    )(*([] if buckets is None else [buckets]), *operands)


def swap(x, axis, bits):
    size = lax.axis_size(axis)
    return lax.ppermute(x, axis, [(i, i ^ bits) for i in range(size)])


def gather(own, axis, ring, side, first=None, loaded=()):
    got = {(0, 0): own}
    got[(0, 1)] = swap(own, axis, side)
    got[(2, 0)] = swap(own, axis, 2 * ring)
    if first is not None:
        got[(2, 0)], first, *loaded = lax.optimization_barrier((got[(2, 0)], first, *loaded))
    got[(1, 0)] = swap(own, axis, ring)
    got[(3, 0)] = swap(own, axis, 3 * ring)
    got[(1, 1)] = swap(got[(0, 1)], axis, ring)
    got[(3, 1)] = swap(got[(0, 1)], axis, 3 * ring)
    got[(2, 1)] = swap(got[(2, 0)], axis, side)
    return [got[rel] for rel in REL], first, loaded


def add(*parts):
    return total(v.astype(F32) for v in parts).astype(BF16)


def scatter(pieces, axis, ring, side, order=FAR + NEAR):
    piece = dict(zip(order, pieces))
    far_1 = swap(piece[(1, 1)], axis, ring)
    far_3 = swap(piece[(3, 1)], axis, 3 * ring)
    far_2 = swap(piece[(2, 1)], axis, side)
    near_1 = swap(piece[(1, 0)], axis, ring)
    near_3 = swap(piece[(3, 0)], axis, 3 * ring)
    near_2 = swap(add(piece[(2, 0)], far_2), axis, 2 * ring)
    crossed = swap(add(piece[(0, 1)], far_1, far_3), axis, side)
    return add(piece[(0, 0)], near_1, near_3, near_2, crossed)


def body(signal, left_factors, right_factors, dense_diagonal, buckets):
    buckets = buckets.T
    right = right_factors[:, 0]
    left = left_factors[:, 0]
    dense = dense_diagonal[0]

    count = signal.shape[0]
    unit = 2 * count * PIECE * PIECE
    size = count * PIECE * 2
    piece = jax.ShapeDtypeStruct((count, PIECE), BF16)
    pair = jax.ShapeDtypeStruct((2, count, PIECE), BF16)
    pair_wide = jax.ShapeDtypeStruct((2, count, PIECE), F32)
    four = jax.ShapeDtypeStruct((4, count, PIECE), BF16)
    eight_wide = jax.ShapeDtypeStruct((8, count, PIECE), F32)

    left_mate = swap(left, "tcol", 1)
    x, left_mate, loaded = gather(signal, "trow", 1, 4, left_mate, load(dense))
    (dense,) = loaded
    (coeff,) = call(coeff_kernel, "coeff", [*x, right], [pair], 16 * unit, 10 * size + 2**21, buckets)
    coeff_mate = swap(coeff, "tcol", 1)
    (dense_sent,) = call(functools.partial(diag_kernel, 1), "diag_mate", [*x, dense], [four], 32 * unit, 12 * size + 2**23)
    dense_mate = swap(dense_sent, "tcol", 1)
    (dense_own,) = call(functools.partial(diag_kernel, 0), "diag_own", [*x, dense], [four], 32 * unit, 12 * size + 2**23)
    terms = []
    for rels in (FAR, NEAR):
        terms += call(
            functools.partial(term_kernel, rels),
            "term",
            [coeff, coeff_mate, left, left_mate, dense_own, dense_mate],
            [piece] * len(rels),
            2 * len(rels) * unit,
            2 * len(rels) * size + 2**21,
        )
    first = scatter(terms, "tcol", 4, 2)
    y, _, _ = gather(first, "tcol", 4, 2)
    (y_sent,) = call(pack_kernel, "pack", y, [four], 0, 12 * size)
    y_mate = swap(y_sent, "tcol", 1)
    own, mate = call(back_kernel, "back", [*y, left, left_mate], [pair_wide, pair], 16 * unit, 14 * size + 2**21)
    mate = swap(mate, "tcol", 1)
    (dense_sum,) = call(diag_back_kernel, "diag_back", [*y, dense], [eight_wide], 32 * unit, 24 * size + 2**22)
    terms = []
    for rels in GROUPS_D:
        terms += call(
            functools.partial(second_kernel, rels),
            "second",
            [own, mate, right, dense_sum, y_mate, dense],
            [piece] * len(rels),
            6 * len(rels) * unit,
            4 * len(rels) * size + 3 * 2**20,
            buckets,
        )
    second = scatter(terms, "trow", 1, 4, sum(GROUPS_D, []))
    return (first, second)


def solution(mesh):
    in_specs = (
        P(None, ("tcol", "trow")),
        P("trow", "tcol", None, None),
        P("trow", "tcol", None, None),
        P("tcol", None, None),
        P("trow", "tcol"),
    )
    out_specs = (P(None, ("trow", "tcol")), P(None, ("tcol", "trow")))
    return jax.shard_map(body, mesh=mesh, in_specs=in_specs, out_specs=out_specs, check_vma=False)
```

```python
import functools

import jax
import jax.numpy as jnp
from jax import lax
from jax.experimental import pallas as pl
from jax.experimental.pallas import tpu as pltpu
from jax.sharding import PartitionSpec as P

PIECE = 256
F32 = jnp.float32
BF16 = jnp.bfloat16
REL = [(d, x) for d in range(4) for x in range(2)]
FAR = [(1, 1), (3, 1), (2, 1)]
NEAR = [(1, 0), (3, 0), (2, 0), (0, 1), (0, 0)]
GROUPS_D = [[(1, 1), (3, 1), (2, 1)], [(2, 0), (0, 1)], [(1, 0), (3, 0), (0, 0)]]
VMEM = pl.BlockSpec(memory_space=pltpu.VMEM)


def dot(a, b):
    return lax.dot_general(a, b, (((1,), (0,)), ((), ())), preferred_element_type=F32)


def dot_t(a, b):
    return lax.dot_general(a, b, (((1,), (1,)), ((), ())), preferred_element_type=F32)


def total(parts):
    return functools.reduce(lambda a, b: a + b, parts)


class Place:
    def __init__(self, buckets=None):
        trow = lax.axis_index("trow")
        tcol = lax.axis_index("tcol")
        self.x_lo, self.z = trow >> 2, trow & 3
        self.y, self.x_hi, self.core = tcol >> 2, (tcol >> 1) & 1, tcol & 1
        self.owner = trow == tcol >> 1
        if buckets is not None:
            self.ranks = [jnp.where(trow * 2 + t == tcol, 0, 16 << buckets[:, t : t + 1]) for t in range(2)]


def row_piece(info, rel):
    return (info.x_lo ^ rel[1]) * 4 + (info.z ^ rel[0])


def half_piece(info, rel):
    return (info.y ^ rel[0]) * 2 + (info.x_hi ^ rel[1])


def rows_of(piece):
    return pl.ds(pl.multiple_of(piece * PIECE, PIECE), PIECE)


def left_rows(info, piece):
    return rows_of((piece % 4) * 2 + info.core)


def masked(values, rank):
    columns = lax.broadcasted_iota(jnp.int32, values.shape, 1)
    return jnp.where(columns < rank, values, 0.0)


def coeff_kernel(buckets, *refs):
    info = Place(buckets)
    x, right, out = refs[:8], refs[8], refs[9]
    for t in range(2):
        acc = total(dot(x[n][...], right[t, rows_of(row_piece(info, rel)), :]) for n, rel in enumerate(REL))
        out[t] = masked(acc, info.ranks[t]).astype(BF16)


def diag_kernel(for_mate, *refs):
    info = Place()
    x, dense, out = refs[:8], refs[8], refs[9]
    parity = info.core ^ for_mate

    @pl.when(info.owner)
    def _():
        for q in range(4):
            rows = rows_of(2 * q + parity)
            acc = total(dot_t(x[n][...], dense[rows, rows_of(row_piece(info, rel))]) for n, rel in enumerate(REL))
            out[q] = acc.astype(out.dtype)


def term_kernel(rels, own, mate, left_own, left_mate, dense_own, dense_mate, *outs):
    info = Place()

    def low(piece):
        tile = piece // 4
        rows = left_rows(info, piece)
        return dot_t(own[tile], left_own[tile, rows, :]) + dot_t(mate[tile], left_mate[tile, rows, :])

    @pl.when(jnp.logical_not(info.owner))
    def _():
        for out, rel in zip(outs, rels):
            out[...] = low(half_piece(info, rel)).astype(BF16)

    @pl.when(info.owner)
    def _():
        for out, rel in zip(outs, rels):
            piece = half_piece(info, rel)
            extra = jnp.where(piece // 4 == info.core, dense_own[piece % 4], dense_mate[piece % 4])
            out[...] = (low(piece) + extra.astype(F32)).astype(BF16)


def pack_kernel(*refs):
    info = Place()
    y, out = refs[:8], refs[8]
    for n, rel in enumerate(REL):
        piece = half_piece(info, rel)

        @pl.when(jnp.logical_and(info.owner, piece // 4 != info.core))
        def _():
            out[piece % 4] = y[n][...]


def back_kernel(*refs):
    info = Place()
    y, left_own, left_mate, own, mate = refs[:8], refs[8], refs[9], refs[10], refs[11]
    for half in range(2):
        tile = (info.y // 2) ^ half
        for left, out in ((left_mate, mate), (left_own, own)):
            out[tile] = total(
                dot(y[n][...], left[tile, left_rows(info, half_piece(info, rel)), :])
                for n, rel in enumerate(REL)
                if rel[0] // 2 == half
            ).astype(out.dtype)


def diag_back_kernel(*refs):
    info = Place()
    y, dense, out = refs[:8], refs[8], refs[9]
    for half in range(2):

        @pl.when(jnp.logical_and(info.owner, (info.y // 2) ^ half == info.core))
        def _():
            for p in range(8):
                out[p] = total(
                    dot(y[n][...], dense[left_rows(info, half_piece(info, rel)), p * PIECE : (p + 1) * PIECE])
                    for n, rel in enumerate(REL)
                    if rel[0] // 2 == half
                )


def second_kernel(rels, buckets, own, mate, right, dense_sum, y_mate, dense, *outs):
    info = Place(buckets)
    coeff = [masked(own[t] + mate[t].astype(F32), info.ranks[t]).astype(BF16) for t in range(2)]

    def low(rows):
        return dot_t(coeff[0], right[0, rows, :]) + dot_t(coeff[1], right[1, rows, :])

    @pl.when(jnp.logical_not(info.owner))
    def _():
        for out, rel in zip(outs, rels):
            out[...] = low(rows_of(row_piece(info, rel))).astype(BF16)

    @pl.when(info.owner)
    def _():
        for out, rel in zip(outs, rels):
            piece = row_piece(info, rel)
            rows = rows_of(piece)
            rest = total(dot(y_mate[q], dense[rows_of(2 * q + 1 - info.core), rows]) for q in range(4))
            out[...] = (low(rows) + dense_sum[piece] + rest).astype(BF16)


def load_kernel(dense, dense_out, sems):
    @pl.when(Place().owner)
    def _():
        blocks = [pltpu.make_async_copy(dense.at[rows_of(p), :], dense_out.at[rows_of(p), :], sems.at[p]) for p in range(8)]
        for block in blocks:
            block.start()
        for block in blocks:
            block.wait()


def load(*arrays):
    return pl.pallas_call(
        load_kernel,
        name="load",
        out_shape=[pltpu.VMEM(v.shape, v.dtype) for v in arrays],
        in_specs=[pl.BlockSpec(memory_space=pltpu.HBM)] * len(arrays),
        out_specs=[VMEM] * len(arrays),
        scratch_shapes=[pltpu.SemaphoreType.DMA((10,))],
        compiler_params=pltpu.CompilerParams(vmem_limit_bytes=16 * 2**20),
        cost_estimate=pl.CostEstimate(flops=0, bytes_accessed=20 * 2**20, transcendentals=0),
    )(*(pltpu.with_memory_space_constraint(v, pltpu.HBM) for v in arrays))


def call(kernel, name, operands, outs, flops, moved, buckets=None):
    return pl.pallas_call(
        kernel,
        name=name,
        out_shape=outs,
        in_specs=[VMEM] * (len(operands) + (buckets is not None)),
        out_specs=[VMEM] * len(outs),
        compiler_params=pltpu.CompilerParams(vmem_limit_bytes=16 * 2**20),
        cost_estimate=pl.CostEstimate(flops=flops, bytes_accessed=moved, transcendentals=0),
    )(*([] if buckets is None else [buckets]), *operands)


def swap(x, axis, bits):
    size = lax.axis_size(axis)
    return lax.ppermute(x, axis, [(i, i ^ bits) for i in range(size)])


def gather(own, axis, ring, side, first=None, loaded=()):
    got = {(0, 0): own}
    got[(0, 1)] = swap(own, axis, side)
    got[(2, 0)] = swap(own, axis, 2 * ring)
    if first is not None:
        got[(2, 0)], first = lax.optimization_barrier((got[(2, 0)], first))
    got[(1, 0)] = swap(own, axis, ring)
    got[(3, 0)] = swap(own, axis, 3 * ring)
    got[(1, 1)] = swap(got[(0, 1)], axis, ring)
    got[(3, 1)] = swap(got[(0, 1)], axis, 3 * ring)
    got[(2, 1)] = swap(got[(2, 0)], axis, side)
    return [got[rel] for rel in REL], first, loaded


def add(*parts):
    return total(v.astype(F32) for v in parts).astype(BF16)


def scatter(pieces, axis, ring, side, order=FAR + NEAR):
    piece = dict(zip(order, pieces))
    far_1 = swap(piece[(1, 1)], axis, ring)
    far_3 = swap(piece[(3, 1)], axis, 3 * ring)
    far_2 = swap(piece[(2, 1)], axis, side)
    near_1 = swap(piece[(1, 0)], axis, ring)
    near_3 = swap(piece[(3, 0)], axis, 3 * ring)
    near_2 = swap(add(piece[(2, 0)], far_2), axis, 2 * ring)
    crossed = swap(add(piece[(0, 1)], far_1, far_3), axis, side)
    return add(piece[(0, 0)], near_1, near_3, near_2, crossed)


def body(signal, left_factors, right_factors, dense_diagonal, buckets):
    buckets = buckets.T
    right = right_factors[:, 0]
    left = left_factors[:, 0]
    dense = dense_diagonal[0]

    count = signal.shape[0]
    unit = 2 * count * PIECE * PIECE
    size = count * PIECE * 2
    piece = jax.ShapeDtypeStruct((count, PIECE), BF16)
    pair = jax.ShapeDtypeStruct((2, count, PIECE), BF16)
    pair_wide = jax.ShapeDtypeStruct((2, count, PIECE), F32)
    four = jax.ShapeDtypeStruct((4, count, PIECE), BF16)
    eight_wide = jax.ShapeDtypeStruct((8, count, PIECE), F32)

    left_mate = swap(left, "tcol", 1)
    x, left_mate, _ = gather(signal, "trow", 1, 4, left_mate)
    x[6], dense = lax.optimization_barrier((x[6], dense))
    (dense,) = load(dense)
    (coeff,) = call(coeff_kernel, "coeff", [*x, right], [pair], 16 * unit, 10 * size + 2**21, buckets)
    coeff_mate = swap(coeff, "tcol", 1)
    (dense_sent,) = call(functools.partial(diag_kernel, 1), "diag_mate", [*x, dense], [four], 32 * unit, 12 * size + 2**23)
    dense_mate = swap(dense_sent, "tcol", 1)
    (dense_own,) = call(functools.partial(diag_kernel, 0), "diag_own", [*x, dense], [four], 32 * unit, 12 * size + 2**23)
    terms = []
    for rels in (FAR, NEAR):
        terms += call(
            functools.partial(term_kernel, rels),
            "term",
            [coeff, coeff_mate, left, left_mate, dense_own, dense_mate],
            [piece] * len(rels),
            2 * len(rels) * unit,
            2 * len(rels) * size + 2**21,
        )
    first = scatter(terms, "tcol", 4, 2)
    y, _, _ = gather(first, "tcol", 4, 2)
    (y_sent,) = call(pack_kernel, "pack", y, [four], 0, 12 * size)
    y_mate = swap(y_sent, "tcol", 1)
    own, mate = call(back_kernel, "back", [*y, left, left_mate], [pair_wide, pair], 16 * unit, 14 * size + 2**21)
    mate = swap(mate, "tcol", 1)
    (dense_sum,) = call(diag_back_kernel, "diag_back", [*y, dense], [eight_wide], 32 * unit, 24 * size + 2**22)
    terms = []
    for rels in GROUPS_D:
        terms += call(
            functools.partial(second_kernel, rels),
            "second",
            [own, mate, right, dense_sum, y_mate, dense],
            [piece] * len(rels),
            6 * len(rels) * unit,
            4 * len(rels) * size + 3 * 2**20,
            buckets,
        )
    second = scatter(terms, "trow", 1, 4, sum(GROUPS_D, []))
    return (first, second)


def solution(mesh):
    in_specs = (
        P(None, ("tcol", "trow")),
        P("trow", "tcol", None, None),
        P("trow", "tcol", None, None),
        P("tcol", None, None),
        P("trow", "tcol"),
    )
    out_specs = (P(None, ("trow", "tcol")), P(None, ("tcol", "trow")))
    return jax.shard_map(body, mesh=mesh, in_specs=in_specs, out_specs=out_specs, check_vma=False)
```

```python
import functools

import jax
import jax.numpy as jnp
from jax import lax
from jax.experimental import pallas as pl
from jax.experimental.pallas import tpu as pltpu
from jax.sharding import PartitionSpec as P

PIECE = 256
F32 = jnp.float32
BF16 = jnp.bfloat16
REL = [(d, x) for d in range(4) for x in range(2)]
FAR = [(1, 1), (3, 1), (2, 1)]
NEAR = [(1, 0), (3, 0), (2, 0), (0, 1), (0, 0)]
GROUPS_D = [[(1, 1), (3, 1), (2, 1)], [(2, 0), (0, 1)], [(1, 0), (3, 0), (0, 0)]]
GROUPS_B = [[(1, 1), (3, 1), (2, 1)], [(2, 0)], [(0, 1), (1, 0), (3, 0), (0, 0)]]
VMEM = pl.BlockSpec(memory_space=pltpu.VMEM)


def dot(a, b):
    return lax.dot_general(a, b, (((1,), (0,)), ((), ())), preferred_element_type=F32)


def dot_t(a, b):
    return lax.dot_general(a, b, (((1,), (1,)), ((), ())), preferred_element_type=F32)


def total(parts):
    return functools.reduce(lambda a, b: a + b, parts)


class Place:
    def __init__(self, buckets=None):
        trow = lax.axis_index("trow")
        tcol = lax.axis_index("tcol")
        self.x_lo, self.z = trow >> 2, trow & 3
        self.y, self.x_hi, self.core = tcol >> 2, (tcol >> 1) & 1, tcol & 1
        self.owner = trow == tcol >> 1
        if buckets is not None:
            self.ranks = [jnp.where(trow * 2 + t == tcol, 0, 16 << buckets[:, t : t + 1]) for t in range(2)]


def row_piece(info, rel):
    return (info.x_lo ^ rel[1]) * 4 + (info.z ^ rel[0])


def half_piece(info, rel):
    return (info.y ^ rel[0]) * 2 + (info.x_hi ^ rel[1])


def rows_of(piece):
    return pl.ds(pl.multiple_of(piece * PIECE, PIECE), PIECE)


def left_rows(info, piece):
    return rows_of((piece % 4) * 2 + info.core)


def masked(values, rank):
    columns = lax.broadcasted_iota(jnp.int32, values.shape, 1)
    return jnp.where(columns < rank, values, 0.0)


def coeff_kernel(buckets, *refs):
    info = Place(buckets)
    x, right, out = refs[:8], refs[8], refs[9]
    for t in range(2):
        acc = total(dot(x[n][...], right[t, rows_of(row_piece(info, rel)), :]) for n, rel in enumerate(REL))
        out[t] = masked(acc, info.ranks[t]).astype(BF16)


def diag_kernel(for_mate, *refs):
    info = Place()
    x, dense, out = refs[:8], refs[8], refs[9]
    parity = info.core ^ for_mate

    @pl.when(info.owner)
    def _():
        for q in range(4):
            rows = rows_of(2 * q + parity)
            acc = total(dot_t(x[n][...], dense[rows, rows_of(row_piece(info, rel))]) for n, rel in enumerate(REL))
            out[q] = acc.astype(out.dtype)


def term_kernel(rels, own, mate, left_own, left_mate, dense_own, dense_mate, *outs):
    info = Place()

    def low(piece):
        tile = piece // 4
        rows = left_rows(info, piece)
        return dot_t(own[tile], left_own[tile, rows, :]) + dot_t(mate[tile], left_mate[tile, rows, :])

    @pl.when(jnp.logical_not(info.owner))
    def _():
        for out, rel in zip(outs, rels):
            out[...] = low(half_piece(info, rel)).astype(BF16)

    @pl.when(info.owner)
    def _():
        for out, rel in zip(outs, rels):
            piece = half_piece(info, rel)
            extra = jnp.where(piece // 4 == info.core, dense_own[piece % 4], dense_mate[piece % 4])
            out[...] = (low(piece) + extra.astype(F32)).astype(BF16)


def pack_kernel(*refs):
    info = Place()
    y, out = refs[:8], refs[8]
    for n, rel in enumerate(REL):
        piece = half_piece(info, rel)

        @pl.when(jnp.logical_and(info.owner, piece // 4 != info.core))
        def _():
            out[piece % 4] = y[n][...]


def back_kernel(*refs):
    info = Place()
    y, left_own, left_mate, own, mate = refs[:8], refs[8], refs[9], refs[10], refs[11]
    for half in range(2):
        tile = (info.y // 2) ^ half
        for left, out in ((left_mate, mate), (left_own, own)):
            out[tile] = total(
                dot(y[n][...], left[tile, left_rows(info, half_piece(info, rel)), :])
                for n, rel in enumerate(REL)
                if rel[0] // 2 == half
            ).astype(out.dtype)


def diag_back_kernel(*refs):
    info = Place()
    y, dense, out = refs[:8], refs[8], refs[9]
    for half in range(2):

        @pl.when(jnp.logical_and(info.owner, (info.y // 2) ^ half == info.core))
        def _():
            for p in range(8):
                out[p] = total(
                    dot(y[n][...], dense[left_rows(info, half_piece(info, rel)), p * PIECE : (p + 1) * PIECE])
                    for n, rel in enumerate(REL)
                    if rel[0] // 2 == half
                )


def second_kernel(rels, buckets, own, mate, right, dense_sum, y_mate, dense, *outs):
    info = Place(buckets)
    coeff = [masked(own[t] + mate[t].astype(F32), info.ranks[t]).astype(BF16) for t in range(2)]

    def low(rows):
        return dot_t(coeff[0], right[0, rows, :]) + dot_t(coeff[1], right[1, rows, :])

    @pl.when(jnp.logical_not(info.owner))
    def _():
        for out, rel in zip(outs, rels):
            out[...] = low(rows_of(row_piece(info, rel))).astype(BF16)

    @pl.when(info.owner)
    def _():
        for out, rel in zip(outs, rels):
            piece = row_piece(info, rel)
            rows = rows_of(piece)
            rest = total(dot(y_mate[q], dense[rows_of(2 * q + 1 - info.core), rows]) for q in range(4))
            out[...] = (low(rows) + dense_sum[piece] + rest).astype(BF16)


def load_kernel(dense, dense_out, sems):
    @pl.when(Place().owner)
    def _():
        blocks = [pltpu.make_async_copy(dense.at[rows_of(p), :], dense_out.at[rows_of(p), :], sems.at[p]) for p in range(8)]
        for block in blocks:
            block.start()
        for block in blocks:
            block.wait()


def load(*arrays):
    return pl.pallas_call(
        load_kernel,
        name="load",
        out_shape=[pltpu.VMEM(v.shape, v.dtype) for v in arrays],
        in_specs=[pl.BlockSpec(memory_space=pltpu.HBM)] * len(arrays),
        out_specs=[VMEM] * len(arrays),
        scratch_shapes=[pltpu.SemaphoreType.DMA((10,))],
        compiler_params=pltpu.CompilerParams(vmem_limit_bytes=16 * 2**20),
        cost_estimate=pl.CostEstimate(flops=0, bytes_accessed=20 * 2**20, transcendentals=0),
    )(*(pltpu.with_memory_space_constraint(v, pltpu.HBM) for v in arrays))


def call(kernel, name, operands, outs, flops, moved, buckets=None):
    return pl.pallas_call(
        kernel,
        name=name,
        out_shape=outs,
        in_specs=[VMEM] * (len(operands) + (buckets is not None)),
        out_specs=[VMEM] * len(outs),
        compiler_params=pltpu.CompilerParams(vmem_limit_bytes=16 * 2**20),
        cost_estimate=pl.CostEstimate(flops=flops, bytes_accessed=moved, transcendentals=0),
    )(*([] if buckets is None else [buckets]), *operands)


def swap(x, axis, bits):
    size = lax.axis_size(axis)
    return lax.ppermute(x, axis, [(i, i ^ bits) for i in range(size)])


def gather(own, axis, ring, side, first=None, loaded=()):
    got = {(0, 0): own}
    got[(0, 1)] = swap(own, axis, side)
    got[(2, 0)] = swap(own, axis, 2 * ring)
    if first is not None:
        got[(2, 0)], first, *loaded = lax.optimization_barrier((got[(2, 0)], first, *loaded))
    got[(1, 0)] = swap(own, axis, ring)
    got[(3, 0)] = swap(own, axis, 3 * ring)
    got[(1, 1)] = swap(got[(0, 1)], axis, ring)
    got[(3, 1)] = swap(got[(0, 1)], axis, 3 * ring)
    got[(2, 1)] = swap(got[(2, 0)], axis, side)
    return [got[rel] for rel in REL], first, loaded


def add(*parts):
    return total(v.astype(F32) for v in parts).astype(BF16)


def scatter(pieces, axis, ring, side, order=FAR + NEAR):
    piece = dict(zip(order, pieces))
    far_1 = swap(piece[(1, 1)], axis, ring)
    far_3 = swap(piece[(3, 1)], axis, 3 * ring)
    far_2 = swap(piece[(2, 1)], axis, side)
    near_1 = swap(piece[(1, 0)], axis, ring)
    near_3 = swap(piece[(3, 0)], axis, 3 * ring)
    near_2 = swap(add(piece[(2, 0)], far_2), axis, 2 * ring)
    crossed = swap(add(piece[(0, 1)], far_1, far_3), axis, side)
    return add(piece[(0, 0)], near_1, near_3, near_2, crossed)


def body(signal, left_factors, right_factors, dense_diagonal, buckets):
    buckets = buckets.T
    right = right_factors[:, 0]
    left = left_factors[:, 0]
    dense = dense_diagonal[0]

    count = signal.shape[0]
    unit = 2 * count * PIECE * PIECE
    size = count * PIECE * 2
    piece = jax.ShapeDtypeStruct((count, PIECE), BF16)
    pair = jax.ShapeDtypeStruct((2, count, PIECE), BF16)
    pair_wide = jax.ShapeDtypeStruct((2, count, PIECE), F32)
    four = jax.ShapeDtypeStruct((4, count, PIECE), BF16)
    eight_wide = jax.ShapeDtypeStruct((8, count, PIECE), F32)

    left_mate = swap(left, "tcol", 1)
    x, left_mate, loaded = gather(signal, "trow", 1, 4, left_mate, load(dense))
    (dense,) = loaded
    (coeff,) = call(coeff_kernel, "coeff", [*x, right], [pair], 16 * unit, 10 * size + 2**21, buckets)
    coeff_mate = swap(coeff, "tcol", 1)
    (dense_sent,) = call(functools.partial(diag_kernel, 1), "diag_mate", [*x, dense], [four], 32 * unit, 12 * size + 2**23)
    dense_mate = swap(dense_sent, "tcol", 1)
    (dense_own,) = call(functools.partial(diag_kernel, 0), "diag_own", [*x, dense], [four], 32 * unit, 12 * size + 2**23)
    terms = []
    for rels in GROUPS_B:
        terms += call(
            functools.partial(term_kernel, rels),
            "term",
            [coeff, coeff_mate, left, left_mate, dense_own, dense_mate],
            [piece] * len(rels),
            2 * len(rels) * unit,
            2 * len(rels) * size + 2**21,
        )
    first = scatter(terms, "tcol", 4, 2, sum(GROUPS_B, []))
    y, _, _ = gather(first, "tcol", 4, 2)
    (y_sent,) = call(pack_kernel, "pack", y, [four], 0, 12 * size)
    y_mate = swap(y_sent, "tcol", 1)
    own, mate = call(back_kernel, "back", [*y, left, left_mate], [pair_wide, pair], 16 * unit, 14 * size + 2**21)
    mate = swap(mate, "tcol", 1)
    (dense_sum,) = call(diag_back_kernel, "diag_back", [*y, dense], [eight_wide], 32 * unit, 24 * size + 2**22)
    terms = []
    for rels in GROUPS_D:
        terms += call(
            functools.partial(second_kernel, rels),
            "second",
            [own, mate, right, dense_sum, y_mate, dense],
            [piece] * len(rels),
            6 * len(rels) * unit,
            4 * len(rels) * size + 3 * 2**20,
            buckets,
        )
    second = scatter(terms, "trow", 1, 4, sum(GROUPS_D, []))
    return (first, second)


def solution(mesh):
    in_specs = (
        P(None, ("tcol", "trow")),
        P("trow", "tcol", None, None),
        P("trow", "tcol", None, None),
        P("tcol", None, None),
        P("trow", "tcol"),
    )
    out_specs = (P(None, ("trow", "tcol")), P(None, ("tcol", "trow")))
    return jax.shard_map(body, mesh=mesh, in_specs=in_specs, out_specs=out_specs, check_vma=False)
```
